128 devices in a mesh: depth: 8 (over y, z_hi), chan: 16 (over z_lo, x, core).
Axes of the slice: x: 4, y: 4, z: 4 (z_hi: 2, z_lo: 2; z = z_hi * 2 + z_lo), core: 2. Of those that a mesh axis runs over, the one named last changes fastest.
Arguments:
- volume: bfloat16 [256, 32, 4096], P('chan', 'depth'), may hold values from -6 to 6
- kernel: bfloat16 [27, 256, 512], P(None, 'chan'), may hold values from -0.109375 to 0.109375
- cotangent: bfloat16 [512, 16, 1024], P('chan', 'depth'), may hold values from -6 to 6
Outputs:
- activated: bfloat16 [512, 16, 1024], P('chan', 'depth')
- grad_volume: bfloat16 [256, 32, 4096], P('chan', 'depth')
- grad_kernel: float32 [27, 256, 512], P(None, 'chan')
The draws below stay inside these ranges and needn't reach their ends.
All inputs are finite; a program needn't handle non-finite values.
Results may differ from the reference program's by a relative error of at most 0.005.
Values may be sent and summed in bfloat16 or wider, within the bound.
A program may use at most 192 MiB of HBM per device.

```python
import jax
import jax.numpy as jnp
from jax import lax

CIN = 256
COUT = 512
HW = 64
OHW = 32
NZ = 32
OZ = 16


def spiked(entries, own_key, source, target, blocks, factor):
    def block_of(position):
        return (jnp.arange(entries.shape[position]) // (entries.shape[position] // blocks)).reshape((-1,) + (1,) * (entries.ndim - 1 - position))

    one_side = jax.random.permutation(own_key, blocks)[block_of(target)]
    far = (block_of(target) + blocks // 2) % blocks
    return jnp.where((block_of(source) == one_side) | (block_of(source) == far), factor * entries, entries)


def block_levels(own_key, shape, split, low, largest):
    level, own = 1.0, jax.random.fold_in(own_key, 6)
    for position, blocks in split:
        heights = jnp.exp(jax.random.uniform(jax.random.fold_in(own, position), (blocks,), jnp.float32, low / len(split), largest / len(split)))
        level = level * jnp.repeat(heights, shape[position] // blocks).reshape([-1 if axis == position else 1 for axis in range(len(shape))])
    return level


def bell_draw(rng, extent, scale, limit, shards=(), kind=jnp.bfloat16):
    values = scale * jax.random.normal(rng, extent, jnp.float32)
    if shards:
        values = values * block_levels(rng, extent, shards, -0.22, 0.18)
    return jnp.clip(values, -limit, limit).astype(kind)


def heavy_noise(rng, dims, spread, limit, pieces, heavy, dtype=jnp.bfloat16):
    values = spread * jax.random.normal(rng, dims, jnp.float32)
    if pieces:
        values = values * block_levels(rng, dims, pieces, -0.22, 0.18)
    return jnp.clip(spiked(values, jax.random.fold_in(rng, 3), *heavy), -limit, limit).astype(dtype)


def setup_inputs(seed: int = 0) -> dict:
    key_of = jax.random.split(jax.random.key(seed), 4)
    return {
        "volume": bell_draw(key_of[0], (CIN, NZ, HW * HW), 1.0, 6.0, ((0, 16), (1, 8))),
        "kernel": heavy_noise(key_of[1], (27, CIN, COUT), (27 * CIN) ** -0.5, 0.109375, ((1, 16),), (1, 2, 16, 2.0)),
        "cotangent": bell_draw(key_of[2], (COUT, OZ, OHW * OHW), 1.0, 6.0, ((0, 16), (1, 8))),
    }


def convolve(signal_in, filters_in):
    return lax.conv_general_dilated(signal_in, filters_in, (2, 2, 2), ((1, 1), (1, 1), (1, 1)), dimension_numbers=('NCDHW', 'OIDHW', 'NCDHW'), precision=lax.Precision.HIGHEST)

def to_grid(flat):
    channels = flat.shape[0]
    planes = flat.shape[1]
    shaped = flat.reshape(channels, planes, 2, 2, OHW, OHW).transpose(0, 1, 4, 2, 5, 3)
    return shaped.reshape(channels, planes, HW, HW)

def from_grid(grid):
    channels = grid.shape[0]
    planes = grid.shape[1]
    shaped = grid.reshape(channels, planes, OHW, 2, OHW, 2).transpose(0, 1, 3, 5, 2, 4)
    return shaped.reshape(channels, planes, HW * HW)

def reference(volume, kernel, cotangent):
    signal = to_grid(volume.astype(jnp.float32)).reshape(1, CIN, NZ, HW, HW)
    filters = kernel.astype(jnp.float32).reshape(3, 3, 3, CIN, COUT).transpose(4, 3, 0, 1, 2)
    preact, pullback = jax.vjp(convolve, signal, filters)
    sigmas = jax.nn.sigmoid(preact)
    activated = (preact * sigmas).astype(jnp.bfloat16)
    upstream = cotangent.astype(jnp.float32).reshape(1, COUT, OZ, OHW, OHW)
    grad_pre = (upstream * sigmas * (1.0 + preact * (1.0 - sigmas))).astype(jnp.bfloat16)
    grad_signal, grad_filters = pullback(grad_pre.astype(jnp.float32))
    grad_volume = from_grid(grad_signal.reshape(CIN, NZ, HW, HW)).astype(jnp.bfloat16)
    grad_kernel = grad_filters.transpose(2, 3, 4, 1, 0).reshape(27, CIN, COUT)
    return (activated.reshape(COUT, OZ, OHW * OHW), grad_volume, grad_kernel)
```

```python
import itertools

import jax
import jax.numpy as jnp
from jax import lax
from jax.experimental import pallas as pl
from jax.experimental.pallas import tpu as pltpu
from jax.sharding import PartitionSpec as P

MESH = pl.DeviceIdType.MESH
BF = jnp.bfloat16
F32 = jnp.float32
SIDE = 32
CELLS = SIDE * SIDE
TAPS = 27
INS = 16
OUTS = 32
ROWS = TAPS * INS
LEVEL = 9 * INS
DEEP = 512
ALL = 512
PIECE = 112
COPIES = 80


def tap_phase(offset):
    if offset == 1:
        return (0, 0)
    if offset == 2:
        return (1, 0)
    return (1, -1)


def taps_2d():
    for row in range(3):
        for col in range(3):
            row_phase, row_step = tap_phase(row)
            col_phase, col_step = tap_phase(col)
            yield 3 * row + col, 2 * row_phase + col_phase, row_step, col_step


def inside(row_step, col_step):
    places = lax.broadcasted_iota(jnp.int32, (INS, CELLS), 1)
    keep = None
    if row_step:
        keep = places >= SIDE
    if col_step:
        col = (places % SIDE) != 0
        keep = col if keep is None else keep & col
    return keep


def dot(left, right, contract):
    return lax.dot_general(left, right, (contract, ((), ())), preferred_element_type=F32)


def body(
    vol, wk, cot, act, gvol, gker,
    low, upper, views, wfull, wt, sib_out, sib_in, acc,
    a1_out, a1_in, a2_out, a2_in, a3_out, a3_in,
    b1_out, b1_in, b2_out, b2_in, b3_out, b3_in,
    grads, back_out, filt, c1_out, c1_in, c2_out, c2_in, c3_out, c3_in, gk16,
    send_sem, recv_sem,
):
    depth = lax.axis_index("depth")
    chan = lax.axis_index("chan")
    y, zh = depth // 2, depth % 2
    zl, x, core = chan // 8, (chan // 2) % 4, chan % 2

    def at_chan(zl_, x_, core_):
        return (depth, zl_ * 8 + x_ * 2 + core_)

    sibling = at_chan(zl, x, 1 - core)
    right = at_chan(zl, (x + 1) % 4, core)
    left = at_chan(zl, (x + 3) % 4, core)
    pair = at_chan(1 - zl, x, core)
    y_right = (((y + 1) % 4) * 2 + zh, chan)
    y_left = (((y + 3) % 4) * 2 + zh, chan)
    y_pair = (y * 2 + 1 - zh, chan)
    above = ((depth + 1) % 8, chan)
    below = ((depth + 7) % 8, chan)
    peers = (sibling, right, left, pair, y_right, y_left, y_pair, above, below)

    barrier = pltpu.get_barrier_semaphore()
    for peer in peers:
        pl.semaphore_signal(barrier, inc=1, device_id=peer, device_id_type=MESH)

    number = itertools.count()
    sent = []

    def push(src, dst, target):
        n = next(number)
        copy = pltpu.make_async_remote_copy(
            src_ref=src, dst_ref=dst, send_sem=send_sem.at[n], recv_sem=recv_sem.at[n],
            device_id=target, device_id_type=MESH,
        )
        copy.start()
        sent.append(copy)
        return copy

    def build(level, plane):
        wide = plane.astype(F32)
        for tap, phase, row_step, col_step in taps_2d():
            view = wide[:, phase * CELLS : (phase + 1) * CELLS]
            amount = -row_step * SIDE - col_step
            if amount:
                view = jnp.where(inside(row_step, col_step), pltpu.roll(view, amount, 1), 0.0)
            start = level * LEVEL + tap * INS
            views[start : start + INS, :] = view.astype(BF)

    wfull[0:ROWS, :] = wk[...]
    wfull[ROWS:DEEP, :] = jnp.zeros((DEEP - ROWS, ALL), BF)
    wfull[...] = wfull[...].T
    for far in range(2):
        for z_rel in range(2):
            for x_rel in range(4):
                block = ((zl + z_rel) % 2) * 8 + ((x + x_rel) % 4) * 2 + (core + far) % 2
                rows = pl.ds(pl.multiple_of(block * OUTS, OUTS), OUTS)
                start = (z_rel * 4 + x_rel) * OUTS
                wt[far, start : start + OUTS, :] = wfull[rows, :]

    pl.semaphore_wait(barrier, len(peers))
    halo = push(vol.at[3], low, above)

    views[5 * LEVEL :, :] = jnp.zeros((views.shape[0] - 5 * LEVEL, CELLS), BF)
    for plane in (1, 2, 3):
        build(plane + 1, vol[plane])

    def partial(q, far):
        first = 2 * LEVEL * q
        return dot(wt[far], views[first : first + DEEP, :], ((1,), (0,)))

    sib_out[1] = partial(1, 1).astype(BF)
    sib_1 = push(sib_out.at[1], sib_in.at[1], sibling)
    acc[1] = partial(1, 0)
    build(1, vol[0])
    halo.wait_recv()
    build(0, jnp.where(depth > 0, low[...], jnp.zeros((), BF)))
    sib_out[0] = partial(0, 1).astype(BF)
    sib_0 = push(sib_out.at[0], sib_in.at[0], sibling)

    def rows_of(z_rel, x_rel):
        start = (z_rel * 4 + x_rel) * OUTS
        return slice(start, start + OUTS)

    sib_1.wait_recv()
    acc[1] = acc[1] + sib_in[1].astype(F32)
    a1_out[0] = acc[1, rows_of(0, 2), :].astype(BF)
    a1_out[1] = acc[1, rows_of(1, 2), :].astype(BF)
    a1_r = push(a1_out.at[0], a1_in.at[0], right)
    a1_l = push(a1_out.at[1], a1_in.at[1], left)
    acc[0] = partial(0, 0)
    sib_0.wait_recv()
    half = 4 * OUTS
    b1_out[...] = (acc[0, half:, :] + sib_in[0, half:, :].astype(F32)).astype(BF)
    b1 = push(b1_out, b1_in, pair)
    acc[0, :half, :] = acc[0, :half, :] + sib_in[0, :half, :].astype(F32)
    a1_r.wait_recv()
    a2_out[0, 0] = (acc[1, rows_of(0, 1), :] + a1_in[0].astype(F32)).astype(BF)
    a2_out[0, 1] = acc[1, rows_of(1, 1), :].astype(BF)
    a2_r = push(a2_out.at[0], a2_in.at[0], right)
    a1_l.wait_recv()
    a2_out[1, 0] = acc[1, rows_of(0, 3), :].astype(BF)
    a2_out[1, 1] = (acc[1, rows_of(1, 3), :] + a1_in[1].astype(F32)).astype(BF)
    a2_l = push(a2_out.at[1], a2_in.at[1], left)
    a2_r.wait_recv()
    a2_l.wait_recv()
    a3_out[...] = (
        acc[1, rows_of(1, 0), :] + a2_in[0, 1].astype(F32) + a2_in[1, 1].astype(F32)
    ).astype(BF)
    a3 = push(a3_out, a3_in, pair)
    b1.wait_recv()
    acc[0, :half, :] = acc[0, :half, :] + b1_in[...].astype(F32)
    cut = OUTS // 2
    b2_out[0] = acc[0, 2 * OUTS : 2 * OUTS + cut, :].astype(BF)
    b2_out[1] = acc[0, 2 * OUTS + cut : 3 * OUTS, :].astype(BF)
    b2_r = push(b2_out.at[0], b2_in.at[0], right)
    b2_l = push(b2_out.at[1], b2_in.at[1], left)
    b2_r.wait_recv()
    b3_out[0, :cut, :] = (acc[0, OUTS : OUTS + cut, :] + b2_in[0].astype(F32)).astype(BF)
    b3_out[0, cut:, :] = acc[0, OUTS + cut : 2 * OUTS, :].astype(BF)
    b3_r = push(b3_out.at[0], b3_in.at[0], right)
    b2_l.wait_recv()
    b3_out[1, :cut, :] = acc[0, 3 * OUTS : 3 * OUTS + cut, :].astype(BF)
    b3_out[1, cut:, :] = (acc[0, 3 * OUTS + cut : 4 * OUTS, :] + b2_in[1].astype(F32)).astype(BF)
    b3_l = push(b3_out.at[1], b3_in.at[1], left)

    def rows_abs(zl_, x_, core_):
        return pl.multiple_of((zl_ * 8 + x_ * 2 + core_) * OUTS, OUTS)

    mine = rows_abs(zl, x, core)

    def activate(q, preact):
        s = 1.0 / (1.0 + jnp.exp(-preact))
        act[q] = (preact * s).astype(BF)
        grad = cot[q].astype(F32) * s * (1.0 + preact * (1.0 - s))
        grads[q, pl.ds(mine, OUTS), :] = grad.astype(BF)

    def spread(q, start, target, rows=OUTS, skip=0):
        place = grads.at[q, pl.ds(pl.multiple_of(start + skip, 16), rows), :]
        return push(place, place, target)

    xl, xr, xo, zo = (x + 3) % 4, (x + 1) % 4, (x + 2) % 4, 1 - zl
    from_sib = []

    def share(q, start):
        from_sib.append(spread(q, start, sibling))

    a3.wait_recv()
    activate(1, acc[1, rows_of(0, 0), :] + a2_in[0, 0].astype(F32) + a2_in[1, 0].astype(F32) + a3_in[...].astype(F32))
    g1_r = spread(1, mine, right)
    g1_l = spread(1, mine, left)
    g1_z = [spread(1, mine, pair)]
    share(1, mine)
    b3_r.wait_recv()
    b3_l.wait_recv()
    activate(0, acc[0, :OUTS, :] + b3_in[0].astype(F32) + b3_in[1].astype(F32))
    g0_z = spread(0, mine, pair)
    g0_r = spread(0, mine, right)
    g0_l = spread(0, mine, left)
    share(0, mine)

    g1_r.wait_recv()
    block = rows_abs(zl, xl, core)
    g1_fr = spread(1, block, right, cut)
    g1_z.append(spread(1, block, pair))
    share(1, block)
    g1_l.wait_recv()
    block = rows_abs(zl, xr, core)
    g1_fl = spread(1, block, left, cut, cut)
    g1_z.append(spread(1, block, pair))
    share(1, block)
    g0_z.wait_recv()
    block = rows_abs(zo, x, core)
    g0_zr = spread(0, block, right)
    g0_zl = spread(0, block, left)
    share(0, block)
    g0_r.wait_recv()
    block = rows_abs(zl, xl, core)
    g0_fr = spread(0, block, right)
    share(0, block)
    g0_l.wait_recv()
    share(0, rows_abs(zl, xr, core))
    g1_fr.wait_recv()
    g1_fl.wait_recv()
    block = rows_abs(zl, xo, core)
    g1_z.append(spread(1, block, pair))
    share(1, block)
    g0_zr.wait_recv()
    share(0, rows_abs(zo, xl, core))
    g0_zl.wait_recv()
    block = rows_abs(zo, xr, core)
    g0_fl = spread(0, block, left)
    share(0, block)
    g0_fr.wait_recv()
    share(0, rows_abs(zl, xo, core))
    g0_fl.wait_recv()
    share(0, rows_abs(zo, xo, core))
    for copy, x_ in zip(g1_z, (x, xl, xr, xo)):
        copy.wait_recv()
        share(1, rows_abs(zo, x_, core))
    for copy in from_sib:
        copy.wait_recv()

    def spatial(columns):
        sums = {}
        for tap, phase, row_step, col_step in taps_2d():
            moved = columns[tap * INS : (tap + 1) * INS, :]
            amount = -row_step * SIDE - col_step
            if amount:
                moved = pltpu.roll(jnp.where(inside(row_step, col_step), moved, 0.0), CELLS - amount, 1)
            sums[phase] = moved if phase not in sums else sums[phase] + moved
        return [sums[phase] for phase in range(4)]

    def columns_of(q, level):
        return spatial(dot(wk[level * LEVEL : (level + 1) * LEVEL, :], grads[q], ((1,), (0,))))

    def phase_cells(phase):
        return slice(phase * CELLS, (phase + 1) * CELLS)

    lowest = columns_of(0, 0)
    for phase in range(4):
        back_out[:, phase_cells(phase)] = lowest[phase].astype(BF)
    back = push(back_out, upper, below)

    filt[0:ROWS, :] = dot(views[0:ROWS, :], grads[0], ((1,), (1,))) + dot(
        views[2 * LEVEL : 2 * LEVEL + ROWS, :], grads[1], ((1,), (1,))
    )
    filt[ROWS:, :] = jnp.zeros((filt.shape[0] - ROWS, ALL), F32)

    def piece(y_rel, part):
        start = pl.multiple_of(((y + y_rel) % 4) * PIECE, PIECE)
        return filt[pl.ds(start, PIECE), part * 256 : part * 256 + 256]

    c1_out[0] = piece(2, 0).astype(BF)
    c1_out[1] = piece(2, 1).astype(BF)
    c1_r = push(c1_out.at[0], c1_in.at[0], y_right)
    c1_l = push(c1_out.at[1], c1_in.at[1], y_left)

    def store_plane(plane, parts, more=None):
        for phase in range(4):
            total = parts[phase] if more is None else parts[phase] + more[phase]
            gvol[plane, :, phase_cells(phase)] = total.astype(BF)

    store_plane(0, columns_of(0, 1))
    c1_r.wait_recv()
    c2_out[0, 0] = (piece(1, 0) + c1_in[0].astype(F32)).astype(BF)
    c2_out[0, 1] = piece(1, 1).astype(BF)
    c2_r = push(c2_out.at[0], c2_in.at[0], y_right)
    c1_l.wait_recv()
    c2_out[1, 0] = piece(3, 0).astype(BF)
    c2_out[1, 1] = (piece(3, 1) + c1_in[1].astype(F32)).astype(BF)
    c2_l = push(c2_out.at[1], c2_in.at[1], y_left)
    store_plane(1, columns_of(0, 2), columns_of(1, 0))
    store_plane(2, columns_of(1, 1))
    c2_r.wait_recv()
    c2_l.wait_recv()
    whole = [piece(0, part) + c2_in[0, part].astype(F32) + c2_in[1, part].astype(F32) for part in range(2)]
    c3_out[...] = jnp.where(zh == 0, whole[1], whole[0]).astype(BF)
    c3 = push(c3_out, c3_in, y_pair)
    own = jnp.where(zh == 0, whole[0], whole[1])
    last = columns_of(1, 2)
    back.wait_recv()
    edge = upper[...].astype(F32)
    edge = jnp.where(depth < 7, edge, 0.0)
    store_plane(3, last, [edge[:, phase_cells(phase)] for phase in range(4)])
    c3.wait_recv()
    gk16[y, zh] = (own + c3_in[...].astype(F32)).astype(BF)

    def pass_on(y_, part, target):
        return push(gk16.at[y_, part], gk16.at[y_, part], target)

    yl, yr, yo = (y + 3) % 4, (y + 1) % 4, (y + 2) % 4
    d_z = pass_on(y, zh, y_pair)
    d_r = pass_on(y, zh, y_right)
    d_l = pass_on(y, zh, y_left)
    d_z.wait_recv()
    e_r = pass_on(y, 1 - zh, y_right)
    e_l = pass_on(y, 1 - zh, y_left)
    d_r.wait_recv()
    f_r = pass_on(yl, zh, y_right)
    d_l.wait_recv()
    e_r.wait_recv()
    e_l.wait_recv()
    f_l = pass_on(yr, 1 - zh, y_left)
    f_r.wait_recv()
    f_l.wait_recv()
    for y_ in range(4):
        rows = min(PIECE, ROWS - y_ * PIECE)
        for part in range(2):
            gker[y_ * PIECE : y_ * PIECE + rows, part * 256 : part * 256 + 256] = gk16[y_, part, :rows, :].astype(F32)
    for copy in sent:
        copy.wait_send()


def on_device(volume, kernel, cotangent):
    planes = volume.transpose(1, 0, 2)
    upstream = cotangent.transpose(1, 0, 2)
    vmem = pl.BlockSpec(memory_space=pltpu.VMEM)
    scratch = [
        ((INS, 4 * CELLS), BF),
        ((INS, 4 * CELLS), BF),
        ((2 * LEVEL + DEEP, CELLS), BF),
        ((ALL, DEEP), BF),
        ((2, ALL // 2, DEEP), BF),
        ((2, ALL // 2, CELLS), BF),
        ((2, ALL // 2, CELLS), BF),
        ((2, ALL // 2, CELLS), F32),
        ((2, OUTS, CELLS), BF),
        ((2, OUTS, CELLS), BF),
        ((2, 2, OUTS, CELLS), BF),
        ((2, 2, OUTS, CELLS), BF),
        ((OUTS, CELLS), BF),
        ((OUTS, CELLS), BF),
        ((4 * OUTS, CELLS), BF),
        ((4 * OUTS, CELLS), BF),
        ((2, OUTS // 2, CELLS), BF),
        ((2, OUTS // 2, CELLS), BF),
        ((2, OUTS, CELLS), BF),
        ((2, OUTS, CELLS), BF),
        ((2, ALL, CELLS), BF),
        ((INS, 4 * CELLS), BF),
        ((4 * PIECE, ALL), F32),
        ((2, PIECE, 256), BF),
        ((2, PIECE, 256), BF),
        ((2, 2, PIECE, 256), BF),
        ((2, 2, PIECE, 256), BF),
        ((PIECE, 256), BF),
        ((PIECE, 256), BF),
        ((4, 2, PIECE, 256), BF),
    ]
    activated, grad_volume, grad_kernel = pl.pallas_call(
        body,
        out_shape=(
            jax.ShapeDtypeStruct((2, OUTS, CELLS), BF),
            jax.ShapeDtypeStruct((4, INS, 4 * CELLS), BF),
            jax.ShapeDtypeStruct((ROWS, ALL), F32),
        ),
        in_specs=[vmem] * 3,
        out_specs=(vmem,) * 3,
        scratch_shapes=[pltpu.VMEM(shape, kind) for shape, kind in scratch]
        + [pltpu.SemaphoreType.DMA((COPIES,)), pltpu.SemaphoreType.DMA((COPIES,))],
        compiler_params=pltpu.CompilerParams(
            collective_id=0, has_side_effects=True, vmem_limit_bytes=48 * 1024 * 1024
        ),
    )(planes, kernel.reshape(ROWS, ALL), upstream)
    return (
        activated.transpose(1, 0, 2),
        grad_volume.transpose(1, 0, 2),
        grad_kernel.reshape(TAPS, INS, ALL),
    )


def solution(mesh):
    return jax.shard_map(
        on_device,
        mesh=mesh,
        in_specs=(P("chan", "depth", None), P(None, "chan", None), P("chan", "depth", None)),
        out_specs=(P("chan", "depth", None), P("chan", "depth", None), P(None, "chan", None)),
        check_vma=False,
    )
```

```python
import itertools

import jax
import jax.numpy as jnp
from jax import lax
from jax.experimental import pallas as pl
from jax.experimental.pallas import tpu as pltpu
from jax.sharding import PartitionSpec as P

MESH = pl.DeviceIdType.MESH
BF = jnp.bfloat16
F32 = jnp.float32
SIDE = 32
CELLS = SIDE * SIDE
TAPS = 27
INS = 16
OUTS = 32
ROWS = TAPS * INS
LEVEL = 9 * INS
DEEP = 512
ALL = 512
HALF = ALL // 2
PIECE = 112
PART = 128
COPIES = 80


def tap_phase(offset):
    if offset == 1:
        return (0, 0)
    if offset == 2:
        return (1, 0)
    return (1, -1)


def taps_2d():
    for row in range(3):
        for col in range(3):
            row_phase, row_step = tap_phase(row)
            col_phase, col_step = tap_phase(col)
            yield 3 * row + col, 2 * row_phase + col_phase, row_step, col_step


def inside(row_step, col_step):
    places = lax.broadcasted_iota(jnp.int32, (INS, CELLS), 1)
    keep = None
    if row_step:
        keep = places >= SIDE
    if col_step:
        col = (places % SIDE) != 0
        keep = col if keep is None else keep & col
    return keep


def dot(left, right, contract):
    return lax.dot_general(left, right, (contract, ((), ())), preferred_element_type=F32)


def body(
    vol, wk, cot, act, gvol, gker,
    low, upper, views, wfull, wt, sib_out, sib_in, acc, rs_out, rs_in,
    grads, back_out, filt, filt_out, filt_in, gk16,
    send_sem, recv_sem,
):
    depth = lax.axis_index("depth")
    chan = lax.axis_index("chan")
    y, zh = depth // 2, depth % 2
    zl, x, core = chan // 8, (chan // 2) % 4, chan % 2

    def at_chan(dz, dx, dc=0):
        return (depth, ((zl + dz) % 2) * 8 + ((x + dx) % 4) * 2 + (core + dc) % 2)

    def at_depth(dz, dy):
        return (((y + dy) % 4) * 2 + (zh + dz) % 2, chan)

    near = [(0, 1), (0, 3), (0, 2)]
    far = [(1, 0), (1, 1), (1, 3), (1, 2)]
    moves = near + far
    sibling = at_chan(0, 0, 1)
    above = ((depth + 1) % 8, chan)
    below = ((depth + 7) % 8, chan)

    barrier = pltpu.get_barrier_semaphore()
    peers = [sibling] + [at_chan(*m) for m in moves] + [at_depth(*m) for m in moves]
    for peer in peers:
        pl.semaphore_signal(barrier, inc=1, device_id=peer, device_id_type=MESH)

    number = itertools.count()
    sent = []

    def push(src, dst, target):
        n = next(number)
        copy = pltpu.make_async_remote_copy(
            src_ref=src, dst_ref=dst, send_sem=send_sem.at[n], recv_sem=recv_sem.at[n],
            device_id=target, device_id_type=MESH,
        )
        copy.start()
        sent.append(copy)
        return copy

    def build(level, plane):
        wide = plane.astype(F32)
        for tap, phase, row_step, col_step in taps_2d():
            view = wide[:, phase * CELLS : (phase + 1) * CELLS]
            amount = -row_step * SIDE - col_step
            if amount:
                view = jnp.where(inside(row_step, col_step), pltpu.roll(view, amount, 1), 0.0)
            start = level * LEVEL + tap * INS
            views[start : start + INS, :] = view.astype(BF)

    wfull[0:ROWS, :] = wk[...]
    wfull[ROWS:DEEP, :] = jnp.zeros((DEEP - ROWS, ALL), BF)
    wfull[...] = wfull[...].T
    for other in range(2):
        for z_rel in range(2):
            for x_rel in range(4):
                block = ((zl + z_rel) % 2) * 8 + ((x + x_rel) % 4) * 2 + (core + other) % 2
                rows = pl.ds(pl.multiple_of(block * OUTS, OUTS), OUTS)
                start = (z_rel * 4 + x_rel) * OUTS
                wt[other, start : start + OUTS, :] = wfull[rows, :]

    pl.semaphore_wait(barrier, len(peers))
    halo = push(vol.at[3], low, above)

    views[5 * LEVEL :, :] = jnp.zeros((views.shape[0] - 5 * LEVEL, CELLS), BF)
    for plane in (1, 2, 3):
        build(plane + 1, vol[plane])

    def partial(q, other):
        first = 2 * LEVEL * q
        return dot(wt[other], views[first : first + DEEP, :], ((1,), (0,)))

    def to_sibling(q):
        sib_out[q] = partial(q, 1).astype(BF)
        return push(sib_out.at[q], sib_in.at[q], sibling)

    def scatter(q, copy):
        copy.wait_recv()
        acc[q] = acc[q] + sib_in[q].astype(F32)
        rs_out[q] = acc[q].astype(BF)
        copies = []
        for n, (dz, dx) in enumerate(moves):
            start = (dz * 4 + dx) * OUTS
            copies.append(push(rs_out.at[q, start : start + OUTS, :], rs_in.at[q, n], at_chan(dz, dx)))
        return copies

    sib_1 = to_sibling(1)
    acc[1] = partial(1, 0)
    scatter_1 = scatter(1, sib_1)
    build(1, vol[0])
    halo.wait_recv()
    build(0, jnp.where(depth > 0, low[...], jnp.zeros((), BF)))
    sib_0 = to_sibling(0)
    acc[0] = partial(0, 0)
    scatter_0 = scatter(0, sib_0)

    def rows_abs(dz, dx):
        return pl.multiple_of((((zl + dz) % 2) * 8 + ((x + dx) % 4) * 2 + core) * OUTS, OUTS)

    def activate(q, copies):
        for copy in copies:
            copy.wait_recv()
        preact = acc[q, 0:OUTS, :]
        for n in range(len(moves)):
            preact = preact + rs_in[q, n].astype(F32)
        s = 1.0 / (1.0 + jnp.exp(-preact))
        act[q] = (preact * s).astype(BF)
        grad = cot[q].astype(F32) * s * (1.0 + preact * (1.0 - s))
        grads[q, pl.ds(rows_abs(0, 0), OUTS), :] = grad.astype(BF)

    def spread(q, start, target):
        place = grads.at[q, pl.ds(start, OUTS), :]
        return push(place, place, target)

    def gather(q):
        copies = {move: spread(q, rows_abs(0, 0), at_chan(*move)) for move in moves}
        return copies, {(0, 0): spread(q, rows_abs(0, 0), sibling)}

    def share(q, gathered, group):
        for dz, dx in group:
            gathered[0][dz, dx].wait_recv()
            gathered[1][dz, dx] = spread(q, rows_abs(dz, -dx), sibling)

    activate(1, scatter_1)
    gathered_1 = gather(1)
    activate(0, scatter_0)
    gathered_0 = gather(0)
    share(1, gathered_1, near)
    share(1, gathered_1, far)
    share(0, gathered_0, near)
    for gathered in (gathered_1, gathered_0):
        for move in [(0, 0)] + near:
            gathered[1][move].wait_recv()

    def filters(part, z):
        columns = pl.ds(pl.multiple_of(z * HALF, HALF), HALF)
        total = dot(views[0:ROWS, :], grads[0, columns, :], ((1,), (1,))) + dot(
            views[2 * LEVEL : 2 * LEVEL + ROWS, :], grads[1, columns, :], ((1,), (1,))
        )
        for side in range(2):
            filt[part, side, 0:ROWS, :] = total[:, side * PART : (side + 1) * PART]
        filt[part, :, ROWS:, :] = jnp.zeros((2, 4 * PIECE - ROWS, PART), F32)
        filt_out[part] = filt[part].astype(BF)
        copies = []
        for n, (dz, dy) in enumerate(moves):
            start = pl.multiple_of(((y + dy) % 4) * PIECE, PIECE)
            src = filt_out.at[part, (zh + dz) % 2, pl.ds(start, PIECE), :]
            copies.append(push(src, filt_in.at[part, n], at_depth(dz, dy)))
        return copies

    def summed(part, copies):
        for copy in copies:
            copy.wait_recv()
        start = pl.multiple_of(y * PIECE, PIECE)
        total = filt[part, zh, pl.ds(start, PIECE), :]
        for n in range(len(moves)):
            total = total + filt_in[part, n].astype(F32)
        gk16[part, y, zh] = total.astype(BF)
        place = gk16.at[part, y, zh]
        return [push(place, place, at_depth(*move)) for move in moves]

    def finish(part, z, copies):
        for copy in copies:
            copy.wait_recv()
        for y_ in range(4):
            rows = min(PIECE, ROWS - y_ * PIECE)
            for side in range(2):
                columns = pl.ds(pl.multiple_of(z * HALF + side * PART, PART), PART)
                gker[y_ * PIECE : y_ * PIECE + rows, columns] = gk16[part, y_, side, :rows, :].astype(F32)

    reduce_0 = filters(0, zl)
    share(0, gathered_0, far)
    for gathered in (gathered_1, gathered_0):
        for move in far:
            gathered[1][move].wait_recv()
    reduce_1 = filters(1, 1 - zl)

    def spatial(columns):
        sums = {}
        for tap, phase, row_step, col_step in taps_2d():
            moved = columns[tap * INS : (tap + 1) * INS, :]
            amount = -row_step * SIDE - col_step
            if amount:
                moved = pltpu.roll(jnp.where(inside(row_step, col_step), moved, 0.0), CELLS - amount, 1)
            sums[phase] = moved if phase not in sums else sums[phase] + moved
        return [sums[phase] for phase in range(4)]

    def columns_of(q, level):
        return spatial(dot(wk[level * LEVEL : (level + 1) * LEVEL, :], grads[q], ((1,), (0,))))

    def phase_cells(phase):
        return slice(phase * CELLS, (phase + 1) * CELLS)

    def store_plane(plane, parts, more=None):
        for phase in range(4):
            total = parts[phase] if more is None else parts[phase] + more[phase]
            gvol[plane, :, phase_cells(phase)] = total.astype(BF)

    lowest = columns_of(0, 0)
    for phase in range(4):
        back_out[:, phase_cells(phase)] = lowest[phase].astype(BF)
    back = push(back_out, upper, below)
    spread_0 = summed(0, reduce_0)
    store_plane(0, columns_of(0, 1))
    store_plane(1, columns_of(0, 2), columns_of(1, 0))
    spread_1 = summed(1, reduce_1)
    store_plane(2, columns_of(1, 1))
    last = columns_of(1, 2)
    back.wait_recv()
    edge = jnp.where(depth < 7, upper[...].astype(F32), 0.0)
    store_plane(3, last, [edge[:, phase_cells(phase)] for phase in range(4)])
    finish(0, zl, spread_0)
    finish(1, 1 - zl, spread_1)
    for copy in sent:
        copy.wait_send()


def on_device(volume, kernel, cotangent):
    planes = volume.transpose(1, 0, 2)
    upstream = cotangent.transpose(1, 0, 2)
    vmem = pl.BlockSpec(memory_space=pltpu.VMEM)
    scratch = [
        ((INS, 4 * CELLS), BF),
        ((INS, 4 * CELLS), BF),
        ((2 * LEVEL + DEEP, CELLS), BF),
        ((ALL, DEEP), BF),
        ((2, HALF, DEEP), BF),
        ((2, HALF, CELLS), BF),
        ((2, HALF, CELLS), BF),
        ((2, HALF, CELLS), F32),
        ((2, HALF, CELLS), BF),
        ((2, 7, OUTS, CELLS), BF),
        ((2, ALL, CELLS), BF),
        ((INS, 4 * CELLS), BF),
        ((2, 2, 4 * PIECE, PART), F32),
        ((2, 2, 4 * PIECE, PART), BF),
        ((2, 7, PIECE, PART), BF),
        ((2, 4, 2, PIECE, PART), BF),
    ]
    activated, grad_volume, grad_kernel = pl.pallas_call(
        body,
        out_shape=(
            jax.ShapeDtypeStruct((2, OUTS, CELLS), BF),
            jax.ShapeDtypeStruct((4, INS, 4 * CELLS), BF),
            jax.ShapeDtypeStruct((ROWS, ALL), F32),
        ),
        in_specs=[vmem] * 3,
        out_specs=(vmem,) * 3,
        scratch_shapes=[pltpu.VMEM(shape, kind) for shape, kind in scratch]
        + [pltpu.SemaphoreType.DMA((COPIES,)), pltpu.SemaphoreType.DMA((COPIES,))],
        compiler_params=pltpu.CompilerParams(
            collective_id=0, has_side_effects=True, vmem_limit_bytes=48 * 1024 * 1024
        ),
    )(planes, kernel.reshape(ROWS, ALL), upstream)
    return (
        activated.transpose(1, 0, 2),
        grad_volume.transpose(1, 0, 2),
        grad_kernel.reshape(TAPS, INS, ALL),
    )


def solution(mesh):
    return jax.shard_map(
        on_device,
        mesh=mesh,
        in_specs=(P("chan", "depth", None), P(None, "chan", None), P("chan", "depth", None)),
        out_specs=(P("chan", "depth", None), P("chan", "depth", None), P(None, "chan", None)),
        check_vma=False,
    )
```

```python
import itertools

import jax
import jax.numpy as jnp
from jax import lax
from jax.experimental import pallas as pl
from jax.experimental.pallas import tpu as pltpu
from jax.sharding import PartitionSpec as P

MESH = pl.DeviceIdType.MESH
BF = jnp.bfloat16
F32 = jnp.float32
SIDE = 32
CELLS = SIDE * SIDE
TAPS = 27
INS = 16
OUTS = 32
ROWS = TAPS * INS
LEVEL = 9 * INS
DEEP = 512
ALL = 512
HALF = ALL // 2
PIECE = 112
PART = 128
COPIES = 80


def tap_phase(offset):
    if offset == 1:
        return (0, 0)
    if offset == 2:
        return (1, 0)
    return (1, -1)


def taps_2d():
    for row in range(3):
        for col in range(3):
            row_phase, row_step = tap_phase(row)
            col_phase, col_step = tap_phase(col)
            yield 3 * row + col, 2 * row_phase + col_phase, row_step, col_step


def inside(row_step, col_step):
    places = lax.broadcasted_iota(jnp.int32, (INS, CELLS), 1)
    keep = None
    if row_step:
        keep = places >= SIDE
    if col_step:
        col = (places % SIDE) != 0
        keep = col if keep is None else keep & col
    return keep


def unpack(src, rows):
    count, group, width = src.shape
    for tile in range(width // 128):
        size = count * group
        block = src[:, :, tile * 128 : tile * 128 + 128].astype(F32)
        rows[tile * size : tile * size + size, :] = block.reshape(size, 128)


def take(rows, count, group, place):
    size = count * group
    tiles = [rows[pl.ds(tile * size + place, count, stride=group), :] for tile in range(rows.shape[0] // size)]
    return jnp.concatenate(tiles, axis=1)


def put(rows, count, group, place, first, value):
    size = count * group
    for tile in range(value.shape[1] // 128):
        start = (first + tile) * size + place
        rows[pl.ds(start, count, stride=group), :] = value[:, tile * 128 : tile * 128 + 128]


def pack(rows, dst):
    count, group, width = dst.shape
    for tile in range(width // 128):
        size = count * group
        block = rows[tile * size : tile * size + size, :].reshape(count, group, 128)
        dst[:, :, tile * 128 : tile * 128 + 128] = block.astype(BF)


def dot(left, right, contract):
    return lax.dot_general(left, right, (contract, ((), ())), preferred_element_type=F32)


def body(
    vol, wk, cot, act, gvol, gker,
    low, upper, top, vol_rows, cot_rows, act_rows, gvol_rows, views, wt, sib_out, sib_in, acc, rs_out, rs_in,
    grads, back_out, filt, filt_out, filt_in, gk16,
    send_sem, recv_sem,
):
    depth = lax.axis_index("depth")
    chan = lax.axis_index("chan")
    y, zh = depth // 2, depth % 2
    zl, x, core = chan // 8, (chan // 2) % 4, chan % 2

    def at_chan(dz, dx, dc=0):
        return (depth, ((zl + dz) % 2) * 8 + ((x + dx) % 4) * 2 + (core + dc) % 2)

    def at_depth(dz, dy):
        return (((y + dy) % 4) * 2 + (zh + dz) % 2, chan)

    near = [(0, 1), (0, 3), (0, 2)]
    far = [(1, 0), (1, 1), (1, 3), (1, 2)]
    moves = near + far
    sibling = at_chan(0, 0, 1)
    above = ((depth + 1) % 8, chan)
    below = ((depth + 7) % 8, chan)

    barrier = pltpu.get_barrier_semaphore()
    peers = [sibling] + [at_chan(*m) for m in moves] + [at_depth(*m) for m in moves]
    for peer in peers:
        pl.semaphore_signal(barrier, inc=1, device_id=peer, device_id_type=MESH)

    number = itertools.count()
    sent = []

    def push(src, dst, target):
        n = next(number)
        copy = pltpu.make_async_remote_copy(
            src_ref=src, dst_ref=dst, send_sem=send_sem.at[n], recv_sem=recv_sem.at[n],
            device_id=target, device_id_type=MESH,
        )
        copy.start()
        sent.append(copy)
        return copy

    def build(level, wide):
        for tap, phase, row_step, col_step in taps_2d():
            view = wide[:, phase * CELLS : (phase + 1) * CELLS]
            amount = -row_step * SIDE - col_step
            if amount:
                view = jnp.where(inside(row_step, col_step), pltpu.roll(view, amount, 1), 0.0)
            start = level * LEVEL + tap * INS
            views[start : start + INS, :] = view.astype(BF)

    unpack(vol, vol_rows)

    def plane(p):
        return take(vol_rows, INS, 4, p)

    top[...] = plane(3).astype(BF)
    pl.semaphore_wait(barrier, len(peers))
    halo = push(top, low, above)

    views[5 * LEVEL :, :] = jnp.zeros((views.shape[0] - 5 * LEVEL, CELLS), BF)
    for p in (1, 2, 3):
        build(p + 1, plane(p))

    for other in range(2):
        row = lax.broadcasted_iota(jnp.int32, (HALF, ALL), 0)
        channel = lax.broadcasted_iota(jnp.int32, (HALF, ALL), 1)
        z_rel, x_rel, within = row // (4 * OUTS), (row // OUTS) % 4, row % OUTS
        wanted = ((zl + z_rel) % 2) * HALF + ((x + x_rel) % 4) * (2 * OUTS) + ((core + other) % 2) * OUTS + within
        select = jnp.where(channel == wanted, 1.0, 0.0).astype(BF)
        wt[other, :, 0:ROWS] = dot(select, wk[...], ((1,), (1,))).astype(BF)
        wt[other, :, ROWS:DEEP] = jnp.zeros((HALF, DEEP - ROWS), BF)

    def partial(q, other):
        first = 2 * LEVEL * q
        return dot(wt[other], views[first : first + DEEP, :], ((1,), (0,)))

    def to_sibling(q):
        sib_out[q] = partial(q, 1).astype(BF)
        return push(sib_out.at[q], sib_in.at[q], sibling)

    def scatter(q, copy):
        copy.wait_recv()
        acc[q] = acc[q] + sib_in[q].astype(F32)
        rs_out[q] = acc[q].astype(BF)
        copies = []
        for n, (dz, dx) in enumerate(moves):
            start = (dz * 4 + dx) * OUTS
            copies.append(push(rs_out.at[q, start : start + OUTS, :], rs_in.at[q, n], at_chan(dz, dx)))
        return copies

    sib_1 = to_sibling(1)
    acc[1] = partial(1, 0)
    scatter_1 = scatter(1, sib_1)
    unpack(cot, cot_rows)
    build(1, plane(0))
    halo.wait_recv()
    build(0, jnp.where(depth > 0, low[...].astype(F32), 0.0))
    sib_0 = to_sibling(0)
    acc[0] = partial(0, 0)
    scatter_0 = scatter(0, sib_0)

    def rows_abs(dz, dx):
        return pl.multiple_of((((zl + dz) % 2) * 8 + ((x + dx) % 4) * 2 + core) * OUTS, OUTS)

    def activate(q, copies):
        for copy in copies:
            copy.wait_recv()
        preact = acc[q, 0:OUTS, :]
        for n in range(len(moves)):
            preact = preact + rs_in[q, n].astype(F32)
        s = 1.0 / (1.0 + jnp.exp(-preact))
        put(act_rows, OUTS, 2, q, 0, preact * s)
        grad = take(cot_rows, OUTS, 2, q) * s * (1.0 + preact * (1.0 - s))
        grads[q, pl.ds(rows_abs(0, 0), OUTS), :] = grad.astype(BF)

    def spread(q, start, target):
        place = grads.at[q, pl.ds(start, OUTS), :]
        return push(place, place, target)

    shared = {0: {}, 1: {}}

    def share(q, move):
        dz, dx = move
        shared[q][move] = spread(q, rows_abs(dz, -dx), sibling)

    pair = at_chan(1, 0)
    across = {}
    activate(1, scatter_1)
    near_1 = {move: spread(1, rows_abs(0, 0), at_chan(*move)) for move in near}
    across[1, 0] = spread(1, rows_abs(0, 0), pair)
    share(1, (0, 0))
    activate(0, scatter_0)
    across_0 = spread(0, rows_abs(0, 0), pair)
    near_0 = {move: spread(0, rows_abs(0, 0), at_chan(*move)) for move in near}
    share(0, (0, 0))
    for move in near:
        near_1[move].wait_recv()
        across[1, move[1]] = spread(1, rows_abs(0, -move[1]), pair)
        share(1, move)
    across_0.wait_recv()
    far_0 = {(1, dx): spread(0, rows_abs(1, 0), at_chan(0, dx)) for _, dx in near}
    share(0, (1, 0))
    across[1, 0].wait_recv()
    share(1, (1, 0))
    for move in near:
        near_0[move].wait_recv()
        share(0, move)
    for q in range(2):
        for move in [(0, 0)] + near:
            shared[q][move].wait_recv()
    pack(act_rows, act)

    def filters(part, z):
        columns = pl.ds(pl.multiple_of(z * HALF, HALF), HALF)
        total = dot(views[0:ROWS, :], grads[0, columns, :], ((1,), (1,))) + dot(
            views[2 * LEVEL : 2 * LEVEL + ROWS, :], grads[1, columns, :], ((1,), (1,))
        )
        for side in range(2):
            filt[part, side, 0:ROWS, :] = total[:, side * PART : (side + 1) * PART]
        filt[part, :, ROWS:, :] = jnp.zeros((2, 4 * PIECE - ROWS, PART), F32)
        filt_out[part] = filt[part].astype(BF)
        copies = []
        for n, (dz, dy) in enumerate(far + near):
            start = pl.multiple_of(((y + dy) % 4) * PIECE, PIECE)
            src = filt_out.at[part, (zh + dz) % 2, pl.ds(start, PIECE), :]
            copies.append(push(src, filt_in.at[part, n], at_depth(dz, dy)))
        return copies

    def summed(part, copies):
        for copy in copies:
            copy.wait_recv()
        start = pl.multiple_of(y * PIECE, PIECE)
        total = filt[part, zh, pl.ds(start, PIECE), :]
        for n in range(len(moves)):
            total = total + filt_in[part, n].astype(F32)
        gk16[part, y, zh] = total.astype(BF)
        place = gk16.at[part, y, zh]
        return [push(place, place, at_depth(*move)) for move in far + near]

    def finish(part, z, copies):
        for copy in copies:
            copy.wait_recv()
        for y_ in range(4):
            rows = min(PIECE, ROWS - y_ * PIECE)
            for side in range(2):
                columns = pl.ds(pl.multiple_of(z * HALF + side * PART, PART), PART)
                gker[y_ * PIECE : y_ * PIECE + rows, columns] = gk16[part, y_, side, :rows, :].astype(F32)

    reduce_0 = filters(0, zl)
    for _, dx in near:
        across[1, dx].wait_recv()
        share(1, (1, dx))
        far_0[1, dx].wait_recv()
        share(0, (1, dx))
    for q in range(2):
        for move in far:
            shared[q][move].wait_recv()
    reduce_1 = filters(1, 1 - zl)

    def spatial(columns):
        sums = {}
        for tap, phase, row_step, col_step in taps_2d():
            moved = columns[tap * INS : (tap + 1) * INS, :]
            amount = -row_step * SIDE - col_step
            if amount:
                moved = pltpu.roll(jnp.where(inside(row_step, col_step), moved, 0.0), CELLS - amount, 1)
            sums[phase] = moved if phase not in sums else sums[phase] + moved
        return [sums[phase] for phase in range(4)]

    def columns_of(q, level):
        return spatial(dot(wk[level * LEVEL : (level + 1) * LEVEL, :], grads[q], ((1,), (0,))))

    def phase_cells(phase):
        return slice(phase * CELLS, (phase + 1) * CELLS)

    def store_plane(plane, parts, more=None):
        for phase in range(4):
            total = parts[phase] if more is None else parts[phase] + more[phase]
            put(gvol_rows, INS, 4, plane, phase * (CELLS // 128), total)

    lowest = columns_of(0, 0)
    for phase in range(4):
        back_out[:, phase_cells(phase)] = lowest[phase].astype(BF)
    back = push(back_out, upper, below)
    spread_0 = summed(0, reduce_0)
    store_plane(0, columns_of(0, 1))
    store_plane(1, columns_of(0, 2), columns_of(1, 0))
    spread_1 = summed(1, reduce_1)
    store_plane(2, columns_of(1, 1))
    last = columns_of(1, 2)
    back.wait_recv()
    edge = jnp.where(depth < 7, upper[...].astype(F32), 0.0)
    store_plane(3, last, [edge[:, phase_cells(phase)] for phase in range(4)])
    pack(gvol_rows, gvol)
    finish(0, zl, spread_0)
    finish(1, 1 - zl, spread_1)
    for copy in sent:
        copy.wait_send()


def store(act, gvol, gker, act_out, gvol_out, gker_out, sems):
    parts = [(act, act_out), (gvol.at[0:8], gvol_out.at[0:8]), (gvol.at[8:16], gvol_out.at[8:16])]
    for first in range(0, ROWS, LEVEL):
        rows = slice(first, first + LEVEL)
        parts.append((gker.at[rows, :], gker_out.at[rows, :]))
    copies = [pltpu.make_async_copy(src, dst, sems.at[n]) for n, (src, dst) in enumerate(parts)]
    for copy in copies:
        copy.start()
    for copy in copies:
        copy.wait()


def on_device(volume, kernel, cotangent):
    vmem = pl.BlockSpec(memory_space=pltpu.VMEM)
    scratch = [
        ((INS, 4 * CELLS), BF),
        ((INS, 4 * CELLS), BF),
        ((INS, 4 * CELLS), BF),
        ((4 * INS * CELLS // 32, 128), F32),
        ((2 * OUTS * CELLS // 128, 128), F32),
        ((2 * OUTS * CELLS // 128, 128), F32),
        ((4 * INS * CELLS // 32, 128), F32),
        ((2 * LEVEL + DEEP, CELLS), BF),
        ((2, HALF, DEEP), BF),
        ((2, HALF, CELLS), BF),
        ((2, HALF, CELLS), BF),
        ((2, HALF, CELLS), F32),
        ((2, HALF, CELLS), BF),
        ((2, 7, OUTS, CELLS), BF),
        ((2, ALL, CELLS), BF),
        ((INS, 4 * CELLS), BF),
        ((2, 2, 4 * PIECE, PART), F32),
        ((2, 2, 4 * PIECE, PART), BF),
        ((2, 7, PIECE, PART), BF),
        ((2, 4, 2, PIECE, PART), BF),
    ]
    activated, grad_volume, grad_kernel = pl.pallas_call(
        body,
        out_shape=(
            jax.ShapeDtypeStruct(cotangent.shape, BF),
            jax.ShapeDtypeStruct(volume.shape, BF),
            jax.ShapeDtypeStruct((ROWS, ALL), F32),
        ),
        in_specs=[vmem] * 3,
        out_specs=(vmem,) * 3,
        scratch_shapes=[pltpu.VMEM(shape, kind) for shape, kind in scratch]
        + [pltpu.SemaphoreType.DMA((COPIES,)), pltpu.SemaphoreType.DMA((COPIES,))],
        compiler_params=pltpu.CompilerParams(
            collective_id=0, has_side_effects=True, vmem_limit_bytes=48 * 1024 * 1024
        ),
    )(volume, kernel.reshape(ROWS, ALL), cotangent)
    whole = pl.BlockSpec(memory_space=pl.ANY)
    results = (activated, grad_volume, grad_kernel)
    activated, grad_volume, grad_kernel = pl.pallas_call(
        store,
        out_shape=tuple(jax.ShapeDtypeStruct(r.shape, r.dtype) for r in results),
        in_specs=[vmem] * 3,
        out_specs=(whole,) * 3,
        scratch_shapes=[pltpu.SemaphoreType.DMA((6,))],
    )(*results)
    return activated, grad_volume, grad_kernel.reshape(TAPS, INS, ALL)


def solution(mesh):
    return jax.shard_map(
        on_device,
        mesh=mesh,
        in_specs=(P("chan", "depth", None), P(None, "chan", None), P("chan", "depth", None)),
        out_specs=(P("chan", "depth", None), P("chan", "depth", None), P(None, "chan", None)),
        check_vma=False,
    )
```

```python
import itertools

import jax
import jax.numpy as jnp
from jax import lax
from jax.experimental import pallas as pl
from jax.experimental.pallas import tpu as pltpu
from jax.sharding import PartitionSpec as P

MESH = pl.DeviceIdType.MESH
BF = jnp.bfloat16
F32 = jnp.float32
SIDE = 32
CELLS = SIDE * SIDE
TAPS = 27
INS = 16
OUTS = 32
ROWS = TAPS * INS
LEVEL = 9 * INS
DEEP = 512
ALL = 512
HALF = ALL // 2
PIECE = 112
PART = 128
COPIES = 80


def tap_phase(offset):
    if offset == 1:
        return (0, 0)
    if offset == 2:
        return (1, 0)
    return (1, -1)


def taps_2d():
    for row in range(3):
        for col in range(3):
            row_phase, row_step = tap_phase(row)
            col_phase, col_step = tap_phase(col)
            yield 3 * row + col, 2 * row_phase + col_phase, row_step, col_step


def inside(row_step, col_step):
    places = lax.broadcasted_iota(jnp.int32, (INS, CELLS), 1)
    keep = None
    if row_step:
        keep = places >= SIDE
    if col_step:
        col = (places % SIDE) != 0
        keep = col if keep is None else keep & col
    return keep


def unpack(src, rows):
    count, group, width = src.shape
    for tile in range(width // 128):
        size = count * group
        block = src[:, :, tile * 128 : tile * 128 + 128].astype(F32)
        rows[tile * size : tile * size + size, :] = block.reshape(size, 128)


def take(rows, count, group, place):
    size = count * group
    tiles = [rows[pl.ds(tile * size + place, count, stride=group), :] for tile in range(rows.shape[0] // size)]
    return jnp.concatenate(tiles, axis=1)


def put(rows, count, group, place, first, value):
    size = count * group
    for tile in range(value.shape[1] // 128):
        start = (first + tile) * size + place
        rows[pl.ds(start, count, stride=group), :] = value[:, tile * 128 : tile * 128 + 128]


def pack(rows, dst):
    count, group, width = dst.shape
    for tile in range(width // 128):
        size = count * group
        block = rows[tile * size : tile * size + size, :].reshape(count, group, 128)
        dst[:, :, tile * 128 : tile * 128 + 128] = block.astype(BF)


def dot(left, right, contract):
    return lax.dot_general(left, right, (contract, ((), ())), preferred_element_type=F32)


def body(
    vol_hbm, wk_hbm, cot_hbm, act_hbm, gvol_hbm, gker_hbm,
    vol, wk, cot, act, gvol, gker,
    low, upper, top, vol_rows, cot_rows, act_rows, gvol_rows, views, wt, sib_out, sib_in, acc, rs_out, rs_in,
    grads, back_out, filt, filt_out, filt_in, gk16,
    send_sem, recv_sem, load_sem, save_sem,
):
    loads = [
        pltpu.make_async_copy(src, dst, load_sem.at[n])
        for n, (src, dst) in enumerate(((vol_hbm, vol), (wk_hbm, wk), (cot_hbm, cot)))
    ]
    for load in loads:
        load.start()
    saves = []

    def save(src, dst):
        copy = pltpu.make_async_copy(src, dst, save_sem.at[len(saves)])
        copy.start()
        saves.append(copy)

    depth = lax.axis_index("depth")
    chan = lax.axis_index("chan")
    y, zh = depth // 2, depth % 2
    zl, x, core = chan // 8, (chan // 2) % 4, chan % 2

    def at_chan(dz, dx, dc=0):
        return (depth, ((zl + dz) % 2) * 8 + ((x + dx) % 4) * 2 + (core + dc) % 2)

    def at_depth(dz, dy):
        return (((y + dy) % 4) * 2 + (zh + dz) % 2, chan)

    near = [(0, 1), (0, 3), (0, 2)]
    far = [(1, 0), (1, 1), (1, 3), (1, 2)]
    moves = near + far
    sibling = at_chan(0, 0, 1)
    above = ((depth + 1) % 8, chan)
    below = ((depth + 7) % 8, chan)

    barrier = pltpu.get_barrier_semaphore()
    peers = [sibling] + [at_chan(*m) for m in moves] + [at_depth(*m) for m in moves]
    for peer in peers:
        pl.semaphore_signal(barrier, inc=1, device_id=peer, device_id_type=MESH)

    number = itertools.count()
    sent = []

    def push(src, dst, target):
        n = next(number)
        copy = pltpu.make_async_remote_copy(
            src_ref=src, dst_ref=dst, send_sem=send_sem.at[n], recv_sem=recv_sem.at[n],
            device_id=target, device_id_type=MESH,
        )
        copy.start()
        sent.append(copy)
        return copy

    def build(level, wide):
        for tap, phase, row_step, col_step in taps_2d():
            view = wide[:, phase * CELLS : (phase + 1) * CELLS]
            amount = -row_step * SIDE - col_step
            if amount:
                view = jnp.where(inside(row_step, col_step), pltpu.roll(view, amount, 1), 0.0)
            start = level * LEVEL + tap * INS
            views[start : start + INS, :] = view.astype(BF)

    loads[0].wait()
    unpack(vol, vol_rows)

    def plane(p):
        return take(vol_rows, INS, 4, p)

    top[...] = plane(3).astype(BF)
    pl.semaphore_wait(barrier, len(peers))
    halo = push(top, low, above)

    views[5 * LEVEL :, :] = jnp.zeros((views.shape[0] - 5 * LEVEL, CELLS), BF)
    for p in (1, 2, 3):
        build(p + 1, plane(p))

    loads[1].wait()
    for other in range(2):
        row = lax.broadcasted_iota(jnp.int32, (HALF, ALL), 0)
        channel = lax.broadcasted_iota(jnp.int32, (HALF, ALL), 1)
        z_rel, x_rel, within = row // (4 * OUTS), (row // OUTS) % 4, row % OUTS
        wanted = ((zl + z_rel) % 2) * HALF + ((x + x_rel) % 4) * (2 * OUTS) + ((core + other) % 2) * OUTS + within
        select = jnp.where(channel == wanted, 1.0, 0.0).astype(BF)
        wt[other, :, 0:ROWS] = dot(select, wk[...], ((1,), (1,))).astype(BF)
        wt[other, :, ROWS:DEEP] = jnp.zeros((HALF, DEEP - ROWS), BF)

    def partial(q, other):
        first = 2 * LEVEL * q
        return dot(wt[other], views[first : first + DEEP, :], ((1,), (0,)))

    def to_sibling(q):
        sib_out[q] = partial(q, 1).astype(BF)
        return push(sib_out.at[q], sib_in.at[q], sibling)

    def scatter(q, copy):
        copy.wait_recv()
        acc[q] = acc[q] + sib_in[q].astype(F32)
        rs_out[q] = acc[q].astype(BF)
        copies = []
        for n, (dz, dx) in enumerate(moves):
            start = (dz * 4 + dx) * OUTS
            copies.append(push(rs_out.at[q, start : start + OUTS, :], rs_in.at[q, n], at_chan(dz, dx)))
        return copies

    sib_1 = to_sibling(1)
    acc[1] = partial(1, 0)
    scatter_1 = scatter(1, sib_1)
    loads[2].wait()
    unpack(cot, cot_rows)
    build(1, plane(0))
    halo.wait_recv()
    build(0, jnp.where(depth > 0, low[...].astype(F32), 0.0))
    sib_0 = to_sibling(0)
    acc[0] = partial(0, 0)
    scatter_0 = scatter(0, sib_0)

    def rows_abs(dz, dx):
        return pl.multiple_of((((zl + dz) % 2) * 8 + ((x + dx) % 4) * 2 + core) * OUTS, OUTS)

    def activate(q, copies):
        for copy in copies:
            copy.wait_recv()
        preact = acc[q, 0:OUTS, :]
        for n in range(len(moves)):
            preact = preact + rs_in[q, n].astype(F32)
        s = 1.0 / (1.0 + jnp.exp(-preact))
        put(act_rows, OUTS, 2, q, 0, preact * s)
        grad = take(cot_rows, OUTS, 2, q) * s * (1.0 + preact * (1.0 - s))
        grads[q, pl.ds(rows_abs(0, 0), OUTS), :] = grad.astype(BF)

    def spread(q, start, target):
        place = grads.at[q, pl.ds(start, OUTS), :]
        return push(place, place, target)

    shared = {0: {}, 1: {}}

    def share(q, move):
        dz, dx = move
        shared[q][move] = spread(q, rows_abs(dz, -dx), sibling)

    pair = at_chan(1, 0)
    across = {}
    activate(1, scatter_1)
    near_1 = {move: spread(1, rows_abs(0, 0), at_chan(*move)) for move in near}
    across[1, 0] = spread(1, rows_abs(0, 0), pair)
    share(1, (0, 0))
    activate(0, scatter_0)
    across_0 = spread(0, rows_abs(0, 0), pair)
    near_0 = {move: spread(0, rows_abs(0, 0), at_chan(*move)) for move in near}
    share(0, (0, 0))
    for move in near:
        near_1[move].wait_recv()
        across[1, move[1]] = spread(1, rows_abs(0, -move[1]), pair)
        share(1, move)
    across_0.wait_recv()
    far_0 = {(1, dx): spread(0, rows_abs(1, 0), at_chan(0, dx)) for _, dx in near}
    share(0, (1, 0))
    across[1, 0].wait_recv()
    share(1, (1, 0))
    for move in near:
        near_0[move].wait_recv()
        share(0, move)
    for q in range(2):
        for move in [(0, 0)] + near:
            shared[q][move].wait_recv()
    pack(act_rows, act)
    save(act, act_hbm)

    def filters(part, z):
        columns = pl.ds(pl.multiple_of(z * HALF, HALF), HALF)
        total = dot(views[0:ROWS, :], grads[0, columns, :], ((1,), (1,))) + dot(
            views[2 * LEVEL : 2 * LEVEL + ROWS, :], grads[1, columns, :], ((1,), (1,))
        )
        for side in range(2):
            filt[part, side, 0:ROWS, :] = total[:, side * PART : (side + 1) * PART]
        filt[part, :, ROWS:, :] = jnp.zeros((2, 4 * PIECE - ROWS, PART), F32)
        filt_out[part] = filt[part].astype(BF)
        copies = []
        for n, (dz, dy) in enumerate(far + near):
            start = pl.multiple_of(((y + dy) % 4) * PIECE, PIECE)
            src = filt_out.at[part, (zh + dz) % 2, pl.ds(start, PIECE), :]
            copies.append(push(src, filt_in.at[part, n], at_depth(dz, dy)))
        return copies

    def summed(part, copies):
        for copy in copies:
            copy.wait_recv()
        start = pl.multiple_of(y * PIECE, PIECE)
        total = filt[part, zh, pl.ds(start, PIECE), :]
        for n in range(len(moves)):
            total = total + filt_in[part, n].astype(F32)
        gk16[part, y, zh] = total.astype(BF)
        place = gk16.at[part, y, zh]
        return [push(place, place, at_depth(*move)) for move in far + near]

    def finish(part, z, copies):
        for copy in copies:
            copy.wait_recv()
        for y_ in range(4):
            rows = min(PIECE, ROWS - y_ * PIECE)
            for side in range(2):
                columns = pl.ds(pl.multiple_of(z * HALF + side * PART, PART), PART)
                gker[y_ * PIECE : y_ * PIECE + rows, columns] = gk16[part, y_, side, :rows, :].astype(F32)
        columns = pl.ds(pl.multiple_of(z * HALF, HALF), HALF)
        save(gker.at[:, columns], gker_hbm.at[:, columns])

    reduce_0 = filters(0, zl)
    for _, dx in near:
        across[1, dx].wait_recv()
        share(1, (1, dx))
        far_0[1, dx].wait_recv()
        share(0, (1, dx))
    for q in range(2):
        for move in far:
            shared[q][move].wait_recv()
    reduce_1 = filters(1, 1 - zl)

    def spatial(columns):
        sums = {}
        for tap, phase, row_step, col_step in taps_2d():
            moved = columns[tap * INS : (tap + 1) * INS, :]
            amount = -row_step * SIDE - col_step
            if amount:
                moved = pltpu.roll(jnp.where(inside(row_step, col_step), moved, 0.0), CELLS - amount, 1)
            sums[phase] = moved if phase not in sums else sums[phase] + moved
        return [sums[phase] for phase in range(4)]

    def columns_of(q, level):
        return spatial(dot(wk[level * LEVEL : (level + 1) * LEVEL, :], grads[q], ((1,), (0,))))

    def phase_cells(phase):
        return slice(phase * CELLS, (phase + 1) * CELLS)

    def store_plane(plane, parts, more=None):
        for phase in range(4):
            total = parts[phase] if more is None else parts[phase] + more[phase]
            put(gvol_rows, INS, 4, plane, phase * (CELLS // 128), total)

    lowest = columns_of(0, 0)
    for phase in range(4):
        back_out[:, phase_cells(phase)] = lowest[phase].astype(BF)
    back = push(back_out, upper, below)
    spread_0 = summed(0, reduce_0)
    store_plane(0, columns_of(0, 1))
    store_plane(1, columns_of(0, 2), columns_of(1, 0))
    spread_1 = summed(1, reduce_1)
    store_plane(2, columns_of(1, 1))
    last = columns_of(1, 2)
    back.wait_recv()
    edge = jnp.where(depth < 7, upper[...].astype(F32), 0.0)
    store_plane(3, last, [edge[:, phase_cells(phase)] for phase in range(4)])
    pack(gvol_rows, gvol)
    save(gvol, gvol_hbm)
    finish(0, zl, spread_0)
    finish(1, 1 - zl, spread_1)
    for copy in sent:
        copy.wait_send()
    for copy in saves:
        copy.wait()


def store(act, gvol, gker, act_out, gvol_out, gker_out, act_in, gvol_in, gker_in, load_sem, save_sem):
    parts = [(act, act_in, act_out)]
    for first in range(0, INS, 8):
        rows = slice(first, first + 8)
        parts.append((gvol.at[rows], gvol_in.at[rows], gvol_out.at[rows]))
    for first in range(0, ROWS, LEVEL):
        rows = slice(first, first + LEVEL)
        parts.append((gker.at[rows, :], gker_in.at[rows, :], gker_out.at[rows, :]))
    loads = [pltpu.make_async_copy(src, mid, load_sem.at[n]) for n, (src, mid, _) in enumerate(parts)]
    saves = [pltpu.make_async_copy(mid, dst, save_sem.at[n]) for n, (_, mid, dst) in enumerate(parts)]
    for load in loads:
        load.start()
    for load, save in zip(loads, saves):
        load.wait()
        save.start()
    for save in saves:
        save.wait()


def on_device(volume, kernel, cotangent):
    scratch = [
        (volume.shape, BF),
        ((ROWS, ALL), BF),
        (cotangent.shape, BF),
        (cotangent.shape, BF),
        (volume.shape, BF),
        ((ROWS, ALL), F32),
        ((INS, 4 * CELLS), BF),
        ((INS, 4 * CELLS), BF),
        ((INS, 4 * CELLS), BF),
        ((4 * INS * CELLS // 32, 128), F32),
        ((2 * OUTS * CELLS // 128, 128), F32),
        ((2 * OUTS * CELLS // 128, 128), F32),
        ((4 * INS * CELLS // 32, 128), F32),
        ((2 * LEVEL + DEEP, CELLS), BF),
        ((2, HALF, DEEP), BF),
        ((2, HALF, CELLS), BF),
        ((2, HALF, CELLS), BF),
        ((2, HALF, CELLS), F32),
        ((2, HALF, CELLS), BF),
        ((2, 7, OUTS, CELLS), BF),
        ((2, ALL, CELLS), BF),
        ((INS, 4 * CELLS), BF),
        ((2, 2, 4 * PIECE, PART), F32),
        ((2, 2, 4 * PIECE, PART), BF),
        ((2, 7, PIECE, PART), BF),
        ((2, 4, 2, PIECE, PART), BF),
    ]
    whole = pl.BlockSpec(memory_space=pl.ANY)
    activated, grad_volume, grad_kernel = pl.pallas_call(
        body,
        out_shape=(
            jax.ShapeDtypeStruct(cotangent.shape, BF),
            jax.ShapeDtypeStruct(volume.shape, BF),
            jax.ShapeDtypeStruct((ROWS, ALL), F32),
        ),
        in_specs=[whole] * 3,
        out_specs=(whole,) * 3,
        scratch_shapes=[pltpu.VMEM(shape, kind) for shape, kind in scratch]
        + [pltpu.SemaphoreType.DMA((COPIES,)), pltpu.SemaphoreType.DMA((COPIES,)), pltpu.SemaphoreType.DMA((3,)), pltpu.SemaphoreType.DMA((4,))],
        compiler_params=pltpu.CompilerParams(
            collective_id=0, has_side_effects=True, vmem_limit_bytes=56 * 1024 * 1024
        ),
    )(volume, kernel.reshape(ROWS, ALL), cotangent)
    results = (activated, grad_volume, grad_kernel)
    activated, grad_volume, grad_kernel = pl.pallas_call(
        store,
        out_shape=tuple(jax.ShapeDtypeStruct(r.shape, r.dtype) for r in results),
        in_specs=[whole] * 3,
        out_specs=(whole,) * 3,
        scratch_shapes=[pltpu.VMEM(r.shape, r.dtype) for r in results]
        + [pltpu.SemaphoreType.DMA((6,)), pltpu.SemaphoreType.DMA((6,))],
        compiler_params=pltpu.CompilerParams(vmem_limit_bytes=56 * 1024 * 1024),
    )(*results)
    return activated, grad_volume, grad_kernel.reshape(TAPS, INS, ALL)


def solution(mesh):
    return jax.shard_map(
        on_device,
        mesh=mesh,
        in_specs=(P("chan", "depth", None), P(None, "chan", None), P("chan", "depth", None)),
        out_specs=(P("chan", "depth", None), P("chan", "depth", None), P(None, "chan", None)),
        check_vma=False,
    )
```

```python
import itertools

import jax
import jax.numpy as jnp
from jax import lax
from jax.experimental import pallas as pl
from jax.experimental.pallas import tpu as pltpu
from jax.sharding import PartitionSpec as P

MESH = pl.DeviceIdType.MESH
BF = jnp.bfloat16
F32 = jnp.float32
SIDE = 32
CELLS = SIDE * SIDE
TAPS = 27
INS = 16
OUTS = 32
ROWS = TAPS * INS
LEVEL = 9 * INS
DEEP = 512
ALL = 512
HALF = ALL // 2
PIECE = 112
PART = 128
COPIES = 80


def tap_phase(offset):
    if offset == 1:
        return (0, 0)
    if offset == 2:
        return (1, 0)
    return (1, -1)


def taps_2d():
    for row in range(3):
        for col in range(3):
            row_phase, row_step = tap_phase(row)
            col_phase, col_step = tap_phase(col)
            yield 3 * row + col, 2 * row_phase + col_phase, row_step, col_step


def inside(row_step, col_step):
    places = lax.broadcasted_iota(jnp.int32, (INS, CELLS), 1)
    keep = None
    if row_step:
        keep = places >= SIDE
    if col_step:
        col = (places % SIDE) != 0
        keep = col if keep is None else keep & col
    return keep


def unpack(src, rows):
    count, group, width = src.shape
    for tile in range(width // 128):
        size = count * group
        block = src[:, :, tile * 128 : tile * 128 + 128].astype(F32)
        rows[tile * size : tile * size + size, :] = block.reshape(size, 128)


def take(rows, count, group, place):
    size = count * group
    tiles = [rows[pl.ds(tile * size + place, count, stride=group), :] for tile in range(rows.shape[0] // size)]
    return jnp.concatenate(tiles, axis=1)


def put(rows, count, group, place, first, value):
    size = count * group
    for tile in range(value.shape[1] // 128):
        start = (first + tile) * size + place
        rows[pl.ds(start, count, stride=group), :] = value[:, tile * 128 : tile * 128 + 128]


def pack(rows, dst):
    count, group, width = dst.shape
    for tile in range(width // 128):
        size = count * group
        block = rows[tile * size : tile * size + size, :].reshape(count, group, 128)
        dst[:, :, tile * 128 : tile * 128 + 128] = block.astype(BF)


def dot(left, right, contract):
    return lax.dot_general(left, right, (contract, ((), ())), preferred_element_type=F32)


def body(
    vol_hbm, wk_hbm, cot_hbm, act_hbm, gvol_hbm, gker_hbm,
    vol, wk, cot, act, gvol, gker,
    low, upper, top, vol_rows, cot_rows, act_rows, gvol_rows, views, wt, sib_out, sib_in, acc, rs_out, rs_in,
    grads, back_out, filt, filt_out, filt_in, gk16,
    send_sem, recv_sem, load_sem, save_sem,
):
    loads = [
        pltpu.make_async_copy(src, dst, load_sem.at[n])
        for n, (src, dst) in enumerate(((vol_hbm, vol), (wk_hbm, wk), (cot_hbm, cot)))
    ]
    for load in loads:
        load.start()
    saves = []

    def save(src, dst):
        copy = pltpu.make_async_copy(src, dst, save_sem.at[len(saves)])
        copy.start()
        saves.append(copy)

    depth = lax.axis_index("depth")
    chan = lax.axis_index("chan")
    y, zh = depth // 2, depth % 2
    zl, x, core = chan // 8, (chan // 2) % 4, chan % 2

    def at_chan(dz, dx, dc=0):
        return (depth, ((zl + dz) % 2) * 8 + ((x + dx) % 4) * 2 + (core + dc) % 2)

    def at_depth(dz, dy):
        return (((y + dy) % 4) * 2 + (zh + dz) % 2, chan)

    near = [(0, 2), (0, 1), (0, 3)]
    far = [(1, 0), (1, 1), (1, 3), (1, 2)]
    moves = near + far
    sibling = at_chan(0, 0, 1)
    above = ((depth + 1) % 8, chan)
    below = ((depth + 7) % 8, chan)

    barrier = pltpu.get_barrier_semaphore()
    peers = [sibling] + [at_chan(*m) for m in moves] + [at_depth(*m) for m in moves]
    for peer in peers:
        pl.semaphore_signal(barrier, inc=1, device_id=peer, device_id_type=MESH)

    number = itertools.count()
    sent = []

    def push(src, dst, target):
        n = next(number)
        copy = pltpu.make_async_remote_copy(
            src_ref=src, dst_ref=dst, send_sem=send_sem.at[n], recv_sem=recv_sem.at[n],
            device_id=target, device_id_type=MESH,
        )
        copy.start()
        sent.append(copy)
        return copy

    def build(level, wide):
        for tap, phase, row_step, col_step in taps_2d():
            view = wide[:, phase * CELLS : (phase + 1) * CELLS]
            amount = -row_step * SIDE - col_step
            if amount:
                view = jnp.where(inside(row_step, col_step), pltpu.roll(view, amount, 1), 0.0)
            start = level * LEVEL + tap * INS
            views[start : start + INS, :] = view.astype(BF)

    loads[0].wait()
    unpack(vol, vol_rows)

    def plane(p):
        return take(vol_rows, INS, 4, p)

    top[...] = plane(3).astype(BF)
    pl.semaphore_wait(barrier, len(peers))
    halo = push(top, low, above)

    views[5 * LEVEL :, :] = jnp.zeros((views.shape[0] - 5 * LEVEL, CELLS), BF)
    for p in (1, 2, 3):
        build(p + 1, plane(p))

    loads[1].wait()
    for other in range(2):
        row = lax.broadcasted_iota(jnp.int32, (HALF, ALL), 0)
        channel = lax.broadcasted_iota(jnp.int32, (HALF, ALL), 1)
        z_rel, x_rel, within = row // (4 * OUTS), (row // OUTS) % 4, row % OUTS
        wanted = ((zl + z_rel) % 2) * HALF + ((x + x_rel) % 4) * (2 * OUTS) + ((core + other) % 2) * OUTS + within
        select = jnp.where(channel == wanted, 1.0, 0.0).astype(BF)
        wt[other, :, 0:ROWS] = dot(select, wk[...], ((1,), (1,))).astype(BF)
        wt[other, :, ROWS:DEEP] = jnp.zeros((HALF, DEEP - ROWS), BF)

    def partial(q, other):
        first = 2 * LEVEL * q
        return dot(wt[other], views[first : first + DEEP, :], ((1,), (0,)))

    def to_sibling(q):
        sib_out[q] = partial(q, 1).astype(BF)
        return push(sib_out.at[q], sib_in.at[q], sibling)

    def scatter(q, copy):
        copy.wait_recv()
        acc[q] = acc[q] + sib_in[q].astype(F32)
        rs_out[q] = acc[q].astype(BF)
        copies = []
        for n, (dz, dx) in enumerate(far + near):
            start = (dz * 4 + dx) * OUTS
            copies.append(push(rs_out.at[q, start : start + OUTS, :], rs_in.at[q, n], at_chan(dz, dx)))
        return copies

    sib_1 = to_sibling(1)
    acc[1] = partial(1, 0)
    scatter_1 = scatter(1, sib_1)
    loads[2].wait()
    unpack(cot, cot_rows)
    build(1, plane(0))
    halo.wait_recv()
    build(0, jnp.where(depth > 0, low[...].astype(F32), 0.0))
    sib_0 = to_sibling(0)
    acc[0] = partial(0, 0)
    scatter_0 = scatter(0, sib_0)

    def rows_abs(dz, dx):
        return pl.multiple_of((((zl + dz) % 2) * 8 + ((x + dx) % 4) * 2 + core) * OUTS, OUTS)

    def activate(q, copies):
        for copy in copies:
            copy.wait_recv()
        preact = acc[q, 0:OUTS, :]
        for n in range(len(moves)):
            preact = preact + rs_in[q, n].astype(F32)
        s = 1.0 / (1.0 + jnp.exp(-preact))
        put(act_rows, OUTS, 2, q, 0, preact * s)
        grad = take(cot_rows, OUTS, 2, q) * s * (1.0 + preact * (1.0 - s))
        grads[q, pl.ds(rows_abs(0, 0), OUTS), :] = grad.astype(BF)

    def spread(q, start, target):
        place = grads.at[q, pl.ds(start, OUTS), :]
        return push(place, place, target)

    shared = {0: {}, 1: {}}

    def share(q, move):
        dz, dx = move
        shared[q][move] = spread(q, rows_abs(dz, -dx), sibling)

    pair = at_chan(1, 0)
    across = {}
    activate(1, scatter_1)
    near_1 = {move: spread(1, rows_abs(0, 0), at_chan(*move)) for move in near}
    across[1, 0] = spread(1, rows_abs(0, 0), pair)
    share(1, (0, 0))
    activate(0, scatter_0)
    across_0 = spread(0, rows_abs(0, 0), pair)
    near_0 = {move: spread(0, rows_abs(0, 0), at_chan(*move)) for move in near}
    share(0, (0, 0))
    for move in near:
        near_1[move].wait_recv()
        across[1, move[1]] = spread(1, rows_abs(0, -move[1]), pair)
        share(1, move)
    across_0.wait_recv()
    far_0 = {(1, dx): spread(0, rows_abs(1, 0), at_chan(0, dx)) for _, dx in near}
    share(0, (1, 0))
    across[1, 0].wait_recv()
    share(1, (1, 0))
    for move in near:
        near_0[move].wait_recv()
        share(0, move)
    for q in range(2):
        for move in [(0, 0)] + near:
            shared[q][move].wait_recv()
    pack(act_rows, act)
    save(act, act_hbm)

    def filters(part, z):
        columns = pl.ds(pl.multiple_of(z * HALF, HALF), HALF)
        total = dot(views[0:ROWS, :], grads[0, columns, :], ((1,), (1,))) + dot(
            views[2 * LEVEL : 2 * LEVEL + ROWS, :], grads[1, columns, :], ((1,), (1,))
        )
        for side in range(2):
            filt[part, side, 0:ROWS, :] = total[:, side * PART : (side + 1) * PART]
        filt[part, :, ROWS:, :] = jnp.zeros((2, 4 * PIECE - ROWS, PART), F32)
        filt_out[part] = filt[part].astype(BF)
        copies = []
        for n, (dz, dy) in enumerate(far + near):
            start = pl.multiple_of(((y + dy) % 4) * PIECE, PIECE)
            src = filt_out.at[part, (zh + dz) % 2, pl.ds(start, PIECE), :]
            copies.append(push(src, filt_in.at[part, n], at_depth(dz, dy)))
        return copies

    def summed(part, copies):
        for copy in copies:
            copy.wait_recv()
        start = pl.multiple_of(y * PIECE, PIECE)
        total = filt[part, zh, pl.ds(start, PIECE), :]
        for n in range(len(moves)):
            total = total + filt_in[part, n].astype(F32)
        gk16[part, y, zh] = total.astype(BF)
        place = gk16.at[part, y, zh]
        return [push(place, place, at_depth(*move)) for move in far + near]

    def finish(part, z, copies):
        for copy in copies:
            copy.wait_recv()
        for y_ in range(4):
            rows = min(PIECE, ROWS - y_ * PIECE)
            for side in range(2):
                columns = pl.ds(pl.multiple_of(z * HALF + side * PART, PART), PART)
                gker[y_ * PIECE : y_ * PIECE + rows, columns] = gk16[part, y_, side, :rows, :].astype(F32)
        columns = pl.ds(pl.multiple_of(z * HALF, HALF), HALF)
        save(gker.at[:, columns], gker_hbm.at[:, columns])

    reduce_0 = filters(0, zl)
    for _, dx in near:
        across[1, dx].wait_recv()
        share(1, (1, dx))
        far_0[1, dx].wait_recv()
        share(0, (1, dx))
    for q in range(2):
        for move in far:
            shared[q][move].wait_recv()
    reduce_1 = filters(1, 1 - zl)
    spread_0 = summed(0, reduce_0)

    def spatial(columns):
        sums = {}
        for tap, phase, row_step, col_step in taps_2d():
            moved = columns[tap * INS : (tap + 1) * INS, :]
            amount = -row_step * SIDE - col_step
            if amount:
                moved = pltpu.roll(jnp.where(inside(row_step, col_step), moved, 0.0), CELLS - amount, 1)
            sums[phase] = moved if phase not in sums else sums[phase] + moved
        return [sums[phase] for phase in range(4)]

    def columns_of(q, level):
        return spatial(dot(wk[level * LEVEL : (level + 1) * LEVEL, :], grads[q], ((1,), (0,))))

    def phase_cells(phase):
        return slice(phase * CELLS, (phase + 1) * CELLS)

    def store_plane(plane, parts, more=None):
        for phase in range(4):
            total = parts[phase] if more is None else parts[phase] + more[phase]
            put(gvol_rows, INS, 4, plane, phase * (CELLS // 128), total)

    lowest = columns_of(0, 0)
    for phase in range(4):
        back_out[:, phase_cells(phase)] = lowest[phase].astype(BF)
    back = push(back_out, upper, below)
    store_plane(0, columns_of(0, 1))
    store_plane(1, columns_of(0, 2), columns_of(1, 0))
    spread_1 = summed(1, reduce_1)
    store_plane(2, columns_of(1, 1))
    last = columns_of(1, 2)
    back.wait_recv()
    edge = jnp.where(depth < 7, upper[...].astype(F32), 0.0)
    store_plane(3, last, [edge[:, phase_cells(phase)] for phase in range(4)])
    pack(gvol_rows, gvol)
    save(gvol, gvol_hbm)
    finish(0, zl, spread_0)
    finish(1, 1 - zl, spread_1)
    for copy in sent:
        copy.wait_send()
    for copy in saves:
        copy.wait()


def store(act, gvol, gker, act_out, gvol_out, gker_out, act_in, gvol_in, gker_in, load_sem, save_sem):
    parts = [(act, act_in, act_out)]
    for first in range(0, INS, 8):
        rows = slice(first, first + 8)
        parts.append((gvol.at[rows], gvol_in.at[rows], gvol_out.at[rows]))
    for first in range(0, ROWS, LEVEL):
        rows = slice(first, first + LEVEL)
        parts.append((gker.at[rows, :], gker_in.at[rows, :], gker_out.at[rows, :]))
    loads = [pltpu.make_async_copy(src, mid, load_sem.at[n]) for n, (src, mid, _) in enumerate(parts)]
    saves = [pltpu.make_async_copy(mid, dst, save_sem.at[n]) for n, (_, mid, dst) in enumerate(parts)]
    for load in loads:
        load.start()
    for load, save in zip(loads, saves):
        load.wait()
        save.start()
    for save in saves:
        save.wait()


def on_device(volume, kernel, cotangent):
    scratch = [
        (volume.shape, BF),
        ((ROWS, ALL), BF),
        (cotangent.shape, BF),
        (cotangent.shape, BF),
        (volume.shape, BF),
        ((ROWS, ALL), F32),
        ((INS, 4 * CELLS), BF),
        ((INS, 4 * CELLS), BF),
        ((INS, 4 * CELLS), BF),
        ((4 * INS * CELLS // 32, 128), F32),
        ((2 * OUTS * CELLS // 128, 128), F32),
        ((2 * OUTS * CELLS // 128, 128), F32),
        ((4 * INS * CELLS // 32, 128), F32),
        ((2 * LEVEL + DEEP, CELLS), BF),
        ((2, HALF, DEEP), BF),
        ((2, HALF, CELLS), BF),
        ((2, HALF, CELLS), BF),
        ((2, HALF, CELLS), F32),
        ((2, HALF, CELLS), BF),
        ((2, 7, OUTS, CELLS), BF),
        ((2, ALL, CELLS), BF),
        ((INS, 4 * CELLS), BF),
        ((2, 2, 4 * PIECE, PART), F32),
        ((2, 2, 4 * PIECE, PART), BF),
        ((2, 7, PIECE, PART), BF),
        ((2, 4, 2, PIECE, PART), BF),
    ]
    whole = pl.BlockSpec(memory_space=pl.ANY)
    activated, grad_volume, grad_kernel = pl.pallas_call(
        body,
        out_shape=(
            jax.ShapeDtypeStruct(cotangent.shape, BF),
            jax.ShapeDtypeStruct(volume.shape, BF),
            jax.ShapeDtypeStruct((ROWS, ALL), F32),
        ),
        in_specs=[whole] * 3,
        out_specs=(whole,) * 3,
        scratch_shapes=[pltpu.VMEM(shape, kind) for shape, kind in scratch]
        + [pltpu.SemaphoreType.DMA((COPIES,)), pltpu.SemaphoreType.DMA((COPIES,)), pltpu.SemaphoreType.DMA((3,)), pltpu.SemaphoreType.DMA((4,))],
        compiler_params=pltpu.CompilerParams(
            collective_id=0, has_side_effects=True, vmem_limit_bytes=56 * 1024 * 1024
        ),
    )(volume, kernel.reshape(ROWS, ALL), cotangent)
    results = (activated, grad_volume, grad_kernel)
    activated, grad_volume, grad_kernel = pl.pallas_call(
        store,
        out_shape=tuple(jax.ShapeDtypeStruct(r.shape, r.dtype) for r in results),
        in_specs=[whole] * 3,
        out_specs=(whole,) * 3,
        scratch_shapes=[pltpu.VMEM(r.shape, r.dtype) for r in results]
        + [pltpu.SemaphoreType.DMA((6,)), pltpu.SemaphoreType.DMA((6,))],
        compiler_params=pltpu.CompilerParams(vmem_limit_bytes=56 * 1024 * 1024),
    )(*results)
    return activated, grad_volume, grad_kernel.reshape(TAPS, INS, ALL)


def solution(mesh):
    return jax.shard_map(
        on_device,
        mesh=mesh,
        in_specs=(P("chan", "depth", None), P(None, "chan", None), P("chan", "depth", None)),
        out_specs=(P("chan", "depth", None), P("chan", "depth", None), P(None, "chan", None)),
        check_vma=False,
    )
```

```python
import itertools

import jax
import jax.numpy as jnp
from jax import lax
from jax.experimental import pallas as pl
from jax.experimental.pallas import tpu as pltpu
from jax.sharding import PartitionSpec as P

MESH = pl.DeviceIdType.MESH
BF = jnp.bfloat16
F32 = jnp.float32
SIDE = 32
CELLS = SIDE * SIDE
TAPS = 27
INS = 16
OUTS = 32
ROWS = TAPS * INS
LEVEL = 9 * INS
DEEP = 512
ALL = 512
HALF = ALL // 2
PIECE = 112
PART = 128
COPIES = 80


def tap_phase(offset):
    if offset == 1:
        return (0, 0)
    if offset == 2:
        return (1, 0)
    return (1, -1)


def taps_2d():
    for row in range(3):
        for col in range(3):
            row_phase, row_step = tap_phase(row)
            col_phase, col_step = tap_phase(col)
            yield 3 * row + col, 2 * row_phase + col_phase, row_step, col_step


def inside(row_step, col_step):
    places = lax.broadcasted_iota(jnp.int32, (INS, CELLS), 1)
    keep = None
    if row_step:
        keep = places >= SIDE
    if col_step:
        col = (places % SIDE) != 0
        keep = col if keep is None else keep & col
    return keep


def unpack(src, rows):
    count, group, width = src.shape
    for tile in range(width // 128):
        size = count * group
        block = src[:, :, tile * 128 : tile * 128 + 128].astype(F32)
        rows[tile * size : tile * size + size, :] = block.reshape(size, 128)


def take(rows, count, group, place):
    size = count * group
    tiles = [rows[pl.ds(tile * size + place, count, stride=group), :] for tile in range(rows.shape[0] // size)]
    return jnp.concatenate(tiles, axis=1)


def put(rows, count, group, place, first, value):
    size = count * group
    for tile in range(value.shape[1] // 128):
        start = (first + tile) * size + place
        rows[pl.ds(start, count, stride=group), :] = value[:, tile * 128 : tile * 128 + 128]


def pack(rows, dst):
    count, group, width = dst.shape
    for tile in range(width // 128):
        size = count * group
        block = rows[tile * size : tile * size + size, :].reshape(count, group, 128)
        dst[:, :, tile * 128 : tile * 128 + 128] = block.astype(BF)


def dot(left, right, contract):
    return lax.dot_general(left, right, (contract, ((), ())), preferred_element_type=F32)


def body(
    vol_hbm, wk_hbm, cot_hbm, act_hbm, gvol_hbm, gker_hbm,
    vol, wk, cot, act, gvol,
    low, upper, top, vol_rows, cot_rows, act_rows, gvol_rows, views, wt, sib_out, sib_in, acc, rs_out, rs_in,
    grads, back_out, filt, filt_out, filt_in, final,
    send_sem, recv_sem, load_sem, save_sem,
):
    loads = [
        pltpu.make_async_copy(src, dst, load_sem.at[n])
        for n, (src, dst) in enumerate(((vol_hbm, vol), (wk_hbm, wk), (cot_hbm, cot)))
    ]
    for load in loads:
        load.start()
    saves = []

    def save(src, dst):
        copy = pltpu.make_async_copy(src, dst, save_sem.at[len(saves)])
        copy.start()
        saves.append(copy)

    depth = lax.axis_index("depth")
    chan = lax.axis_index("chan")
    y, zh = depth // 2, depth % 2
    zl, x, core = chan // 8, (chan // 2) % 4, chan % 2

    def at_chan(dz, dx, dc=0):
        return (depth, ((zl + dz) % 2) * 8 + ((x + dx) % 4) * 2 + (core + dc) % 2)

    def at_depth(dz, dy):
        return (((y + dy) % 4) * 2 + (zh + dz) % 2, chan)

    near = [(0, 2), (0, 1), (0, 3)]
    far = [(1, 0), (1, 1), (1, 3), (1, 2)]
    moves = near + far
    sibling = at_chan(0, 0, 1)

    def by_core(first, second):
        return [(a[0] + core * (b[0] - a[0]), a[1] + core * (b[1] - a[1])) for a, b in zip(first, second)]

    above = ((depth + 1) % 8, chan)
    below = ((depth + 7) % 8, chan)

    barrier = pltpu.get_barrier_semaphore()
    peers = [sibling] + [at_chan(*m) for m in moves] + [at_depth(*m) for m in moves]
    for peer in peers:
        pl.semaphore_signal(barrier, inc=1, device_id=peer, device_id_type=MESH)

    number = itertools.count()
    sent = []

    def push(src, dst, target):
        n = next(number)
        copy = pltpu.make_async_remote_copy(
            src_ref=src, dst_ref=dst, send_sem=send_sem.at[n], recv_sem=recv_sem.at[n],
            device_id=target, device_id_type=MESH,
        )
        copy.start()
        sent.append(copy)
        return copy

    def build(level, wide):
        for tap, phase, row_step, col_step in taps_2d():
            view = wide[:, phase * CELLS : (phase + 1) * CELLS]
            amount = -row_step * SIDE - col_step
            if amount:
                view = jnp.where(inside(row_step, col_step), pltpu.roll(view, amount, 1), 0.0)
            start = level * LEVEL + tap * INS
            views[start : start + INS, :] = view.astype(BF)

    loads[0].wait()
    unpack(vol, vol_rows)

    def plane(p):
        return take(vol_rows, INS, 4, p)

    top[...] = plane(3).astype(BF)
    pl.semaphore_wait(barrier, len(peers))
    halo = push(top, low, above)

    views[5 * LEVEL :, :] = jnp.zeros((views.shape[0] - 5 * LEVEL, CELLS), BF)
    for p in (1, 2, 3):
        build(p + 1, plane(p))

    loads[1].wait()
    for other in range(2):
        row = lax.broadcasted_iota(jnp.int32, (HALF, ALL), 0)
        channel = lax.broadcasted_iota(jnp.int32, (HALF, ALL), 1)
        z_rel, x_rel, within = row // (4 * OUTS), (row // OUTS) % 4, row % OUTS
        wanted = ((zl + z_rel) % 2) * HALF + ((x + x_rel) % 4) * (2 * OUTS) + ((core + other) % 2) * OUTS + within
        select = jnp.where(channel == wanted, 1.0, 0.0).astype(BF)
        wt[other, :, 0:ROWS] = dot(select, wk[...], ((1,), (1,))).astype(BF)
        wt[other, :, ROWS:DEEP] = jnp.zeros((HALF, DEEP - ROWS), BF)

    def partial(q, other):
        first = 2 * LEVEL * q
        return dot(wt[other], views[first : first + DEEP, :], ((1,), (0,)))

    def to_sibling(q):
        sib_out[q] = partial(q, 1).astype(BF)
        return push(sib_out.at[q], sib_in.at[q], sibling)

    def scatter(q, copy):
        copy.wait_recv()
        acc[q] = acc[q] + sib_in[q].astype(F32)
        rs_out[q] = acc[q].astype(BF)
        copies = []
        for n, (dz, dx) in enumerate(by_core(far + near, near + far)):
            start = pl.multiple_of((dz * 4 + dx) * OUTS, OUTS)
            copies.append(push(rs_out.at[q, pl.ds(start, OUTS), :], rs_in.at[q, n], at_chan(dz, dx)))
        return copies

    sib_1 = to_sibling(1)
    acc[1] = partial(1, 0)
    scatter_1 = scatter(1, sib_1)
    loads[2].wait()
    unpack(cot, cot_rows)
    build(1, plane(0))
    halo.wait_recv()
    build(0, jnp.where(depth > 0, low[...].astype(F32), 0.0))
    sib_0 = to_sibling(0)
    acc[0] = partial(0, 0)
    scatter_0 = scatter(0, sib_0)

    def rows_abs(dz, dx):
        return pl.multiple_of((((zl + dz) % 2) * 8 + ((x + dx) % 4) * 2 + core) * OUTS, OUTS)

    def activate(q, copies):
        for copy in copies:
            copy.wait_recv()
        preact = acc[q, 0:OUTS, :]
        for n in range(len(moves)):
            preact = preact + rs_in[q, n].astype(F32)
        s = 1.0 / (1.0 + jnp.exp(-preact))
        put(act_rows, OUTS, 2, q, 0, preact * s)
        grad = take(cot_rows, OUTS, 2, q) * s * (1.0 + preact * (1.0 - s))
        grads[q, pl.ds(rows_abs(0, 0), OUTS), :] = grad.astype(BF)

    def spread(q, start, target):
        place = grads.at[q, pl.ds(start, OUTS), :]
        return push(place, place, target)

    shared = {0: {}, 1: {}}

    def share(q, move):
        dz, dx = move
        shared[q][move] = spread(q, rows_abs(dz, -dx), sibling)

    pair = at_chan(1, 0)
    across = {}
    activate(1, scatter_1)
    near_1 = {move: spread(1, rows_abs(0, 0), at_chan(*move)) for move in near}
    across[1, 0] = spread(1, rows_abs(0, 0), pair)
    share(1, (0, 0))
    activate(0, scatter_0)
    across_0 = spread(0, rows_abs(0, 0), pair)
    near_0 = {move: spread(0, rows_abs(0, 0), at_chan(*move)) for move in near}
    share(0, (0, 0))
    for move in near:
        near_1[move].wait_recv()
        across[1, move[1]] = spread(1, rows_abs(0, -move[1]), pair)
        share(1, move)
    across_0.wait_recv()
    far_0 = {(1, dx): spread(0, rows_abs(1, 0), at_chan(0, dx)) for _, dx in near}
    share(0, (1, 0))
    across[1, 0].wait_recv()
    share(1, (1, 0))
    for move in near:
        near_0[move].wait_recv()
        share(0, move)
    for q in range(2):
        for move in [(0, 0)] + near:
            shared[q][move].wait_recv()
    pack(act_rows, act)
    save(act, act_hbm)

    def filters(part, z):
        columns = pl.ds(pl.multiple_of(z * HALF, HALF), HALF)
        total = dot(views[0:ROWS, :], grads[0, columns, :], ((1,), (1,))) + dot(
            views[2 * LEVEL : 2 * LEVEL + ROWS, :], grads[1, columns, :], ((1,), (1,))
        )
        for side in range(2):
            filt[part, side, 0:ROWS, :] = total[:, side * PART : (side + 1) * PART]
        filt[part, :, ROWS:, :] = jnp.zeros((2, 4 * PIECE - ROWS, PART), F32)
        filt_out[part] = filt[part].astype(BF)
        copies = []
        for n, (dz, dy) in enumerate(far + near):
            start = pl.multiple_of(((y + dy) % 4) * PIECE, PIECE)
            src = filt_out.at[part, (zh + dz) % 2, pl.ds(start, PIECE), :]
            copies.append(push(src, filt_in.at[part, n], at_depth(dz, dy)))
        return copies

    def summed(part, z, copies):
        for copy in copies:
            copy.wait_recv()
        start = pl.multiple_of(y * PIECE, PIECE)
        total = filt[part, zh, pl.ds(start, PIECE), :]
        for n in range(len(moves)):
            total = total + filt_in[part, n].astype(F32)
        final[part] = total.astype(BF)
        place = gker_hbm.at[z, y, zh]
        save(final.at[part], place)
        return [push(final.at[part], place, at_depth(*move)) for move in far + near]

    reduce_0 = filters(0, zl)
    for _, dx in near:
        across[1, dx].wait_recv()
        share(1, (1, dx))
        far_0[1, dx].wait_recv()
        share(0, (1, dx))
    for q in range(2):
        for move in far:
            shared[q][move].wait_recv()
    reduce_1 = filters(1, 1 - zl)
    spread_0 = summed(0, zl, reduce_0)

    def spatial(columns):
        sums = {}
        for tap, phase, row_step, col_step in taps_2d():
            moved = columns[tap * INS : (tap + 1) * INS, :]
            amount = -row_step * SIDE - col_step
            if amount:
                moved = pltpu.roll(jnp.where(inside(row_step, col_step), moved, 0.0), CELLS - amount, 1)
            sums[phase] = moved if phase not in sums else sums[phase] + moved
        return [sums[phase] for phase in range(4)]

    def columns_of(q, level):
        return spatial(dot(wk[level * LEVEL : (level + 1) * LEVEL, :], grads[q], ((1,), (0,))))

    def phase_cells(phase):
        return slice(phase * CELLS, (phase + 1) * CELLS)

    def store_plane(plane, parts, more=None):
        for phase in range(4):
            total = parts[phase] if more is None else parts[phase] + more[phase]
            put(gvol_rows, INS, 4, plane, phase * (CELLS // 128), total)

    lowest = columns_of(0, 0)
    for phase in range(4):
        back_out[:, phase_cells(phase)] = lowest[phase].astype(BF)
    back = push(back_out, upper, below)
    store_plane(0, columns_of(0, 1))
    store_plane(1, columns_of(0, 2), columns_of(1, 0))
    spread_1 = summed(1, 1 - zl, reduce_1)
    store_plane(2, columns_of(1, 1))
    last = columns_of(1, 2)
    back.wait_recv()
    edge = jnp.where(depth < 7, upper[...].astype(F32), 0.0)
    store_plane(3, last, [edge[:, phase_cells(phase)] for phase in range(4)])
    pack(gvol_rows, gvol)
    save(gvol, gvol_hbm)
    for copy in spread_0 + spread_1:
        copy.wait_recv()
    for copy in sent:
        copy.wait_send()
    for copy in saves:
        copy.wait()


def store(act, gvol, pieces, act_out, gvol_out, gker_out, act_in, gvol_in, pieces_in, gker, load_sem, save_sem):
    loads, saves = [], []

    def carry(src, dst, sems, copies):
        copy = pltpu.make_async_copy(src, dst, sems.at[len(copies)])
        copy.start()
        copies.append(copy)

    for z in range(2):
        carry(pieces.at[z], pieces_in.at[z], load_sem, loads)
    carry(gvol, gvol_in, load_sem, loads)
    carry(act, act_in, load_sem, loads)
    for z in range(2):
        loads[z].wait()
        for y in range(4):
            rows = min(PIECE, ROWS - y * PIECE)
            for side in range(2):
                first = z * HALF + side * PART
                gker[y * PIECE : y * PIECE + rows, first : first + PART] = pieces_in[z, y, side, :rows, :].astype(F32)
        columns = slice(z * HALF, (z + 1) * HALF)
        carry(gker.at[:, columns], gker_out.at[:, columns], save_sem, saves)
    loads[2].wait()
    carry(gvol_in, gvol_out, save_sem, saves)
    loads[3].wait()
    carry(act_in, act_out, save_sem, saves)
    for copy in saves:
        copy.wait()


def on_device(volume, kernel, cotangent):
    scratch = [
        (volume.shape, BF),
        ((ROWS, ALL), BF),
        (cotangent.shape, BF),
        (cotangent.shape, BF),
        (volume.shape, BF),
        ((INS, 4 * CELLS), BF),
        ((INS, 4 * CELLS), BF),
        ((INS, 4 * CELLS), BF),
        ((4 * INS * CELLS // 32, 128), F32),
        ((2 * OUTS * CELLS // 128, 128), F32),
        ((2 * OUTS * CELLS // 128, 128), F32),
        ((4 * INS * CELLS // 32, 128), F32),
        ((2 * LEVEL + DEEP, CELLS), BF),
        ((2, HALF, DEEP), BF),
        ((2, HALF, CELLS), BF),
        ((2, HALF, CELLS), BF),
        ((2, HALF, CELLS), F32),
        ((2, HALF, CELLS), BF),
        ((2, 7, OUTS, CELLS), BF),
        ((2, ALL, CELLS), BF),
        ((INS, 4 * CELLS), BF),
        ((2, 2, 4 * PIECE, PART), F32),
        ((2, 2, 4 * PIECE, PART), BF),
        ((2, 7, PIECE, PART), BF),
        ((2, PIECE, PART), BF),
    ]
    whole = pl.BlockSpec(memory_space=pl.ANY)
    activated, grad_volume, grad_kernel = pl.pallas_call(
        body,
        out_shape=(
            jax.ShapeDtypeStruct(cotangent.shape, BF),
            jax.ShapeDtypeStruct(volume.shape, BF),
            jax.ShapeDtypeStruct((2, 4, 2, PIECE, PART), BF),
        ),
        in_specs=[whole] * 3,
        out_specs=(whole,) * 3,
        scratch_shapes=[pltpu.VMEM(shape, kind) for shape, kind in scratch]
        + [pltpu.SemaphoreType.DMA((COPIES,)), pltpu.SemaphoreType.DMA((COPIES,)), pltpu.SemaphoreType.DMA((3,)), pltpu.SemaphoreType.DMA((4,))],
        compiler_params=pltpu.CompilerParams(
            collective_id=0, has_side_effects=True, vmem_limit_bytes=56 * 1024 * 1024
        ),
    )(volume, kernel.reshape(ROWS, ALL), cotangent)
    results = (activated, grad_volume, grad_kernel)
    activated, grad_volume, grad_kernel = pl.pallas_call(
        store,
        out_shape=(
            jax.ShapeDtypeStruct(cotangent.shape, BF),
            jax.ShapeDtypeStruct(volume.shape, BF),
            jax.ShapeDtypeStruct((ROWS, ALL), F32),
        ),
        in_specs=[whole] * 3,
        out_specs=(whole,) * 3,
        scratch_shapes=[pltpu.VMEM(r.shape, r.dtype) for r in results]
        + [pltpu.VMEM((ROWS, ALL), F32), pltpu.SemaphoreType.DMA((4,)), pltpu.SemaphoreType.DMA((4,))],
        compiler_params=pltpu.CompilerParams(vmem_limit_bytes=56 * 1024 * 1024),
    )(*results)
    return activated, grad_volume, grad_kernel.reshape(TAPS, INS, ALL)


def solution(mesh):
    return jax.shard_map(
        on_device,
        mesh=mesh,
        in_specs=(P("chan", "depth", None), P(None, "chan", None), P("chan", "depth", None)),
        out_specs=(P("chan", "depth", None), P("chan", "depth", None), P(None, "chan", None)),
        check_vma=False,
    )
```

```python
import itertools

import jax
import jax.numpy as jnp
from jax import lax
from jax.experimental import pallas as pl
from jax.experimental.pallas import tpu as pltpu
from jax.sharding import PartitionSpec as P

MESH = pl.DeviceIdType.MESH
BF = jnp.bfloat16
F32 = jnp.float32
SIDE = 32
CELLS = SIDE * SIDE
TAPS = 27
INS = 16
OUTS = 32
ROWS = TAPS * INS
LEVEL = 9 * INS
DEEP = 512
ALL = 512
HALF = ALL // 2
PIECE = 112
PART = 128
COPIES = 80


def tap_phase(offset):
    if offset == 1:
        return (0, 0)
    if offset == 2:
        return (1, 0)
    return (1, -1)


def taps_2d():
    for row in range(3):
        for col in range(3):
            row_phase, row_step = tap_phase(row)
            col_phase, col_step = tap_phase(col)
            yield 3 * row + col, 2 * row_phase + col_phase, row_step, col_step


def inside(row_step, col_step):
    places = lax.broadcasted_iota(jnp.int32, (INS, CELLS), 1)
    keep = None
    if row_step:
        keep = places >= SIDE
    if col_step:
        col = (places % SIDE) != 0
        keep = col if keep is None else keep & col
    return keep


def unpack(src, rows):
    count, group, width = src.shape
    for tile in range(width // 128):
        size = count * group
        block = src[:, :, tile * 128 : tile * 128 + 128].astype(F32)
        rows[tile * size : tile * size + size, :] = block.reshape(size, 128)


def take(rows, count, group, place):
    size = count * group
    tiles = [rows[pl.ds(tile * size + place, count, stride=group), :] for tile in range(rows.shape[0] // size)]
    return jnp.concatenate(tiles, axis=1)


def put(rows, count, group, place, first, value):
    size = count * group
    for tile in range(value.shape[1] // 128):
        start = (first + tile) * size + place
        rows[pl.ds(start, count, stride=group), :] = value[:, tile * 128 : tile * 128 + 128]


def pack(rows, dst):
    count, group, width = dst.shape
    for tile in range(width // 128):
        size = count * group
        block = rows[tile * size : tile * size + size, :].reshape(count, group, 128)
        dst[:, :, tile * 128 : tile * 128 + 128] = block.astype(BF)


def dot(left, right, contract):
    return lax.dot_general(left, right, (contract, ((), ())), preferred_element_type=F32)


def body(
    vol_hbm, wk_hbm, cot_hbm, act_hbm, gvol_hbm, gker_hbm,
    vol, wk, cot, act, gvol,
    low, upper, top, vol_rows, cot_rows, act_rows, gvol_rows, views, wt, sib_out, sib_in, acc, rs_out, rs_in,
    grads, back_out, filt, filt_out, filt_in, final,
    send_sem, recv_sem, load_sem, save_sem,
):
    loads = [
        pltpu.make_async_copy(src, dst, load_sem.at[n])
        for n, (src, dst) in enumerate(((vol_hbm, vol), (wk_hbm, wk), (cot_hbm, cot)))
    ]
    for load in loads:
        load.start()
    saves = []

    def save(src, dst):
        copy = pltpu.make_async_copy(src, dst, save_sem.at[len(saves)])
        copy.start()
        saves.append(copy)

    depth = lax.axis_index("depth")
    chan = lax.axis_index("chan")
    y, zh = depth // 2, depth % 2
    zl, x, core = chan // 8, (chan // 2) % 4, chan % 2

    def at_chan(dz, dx, dc=0):
        return (depth, ((zl + dz) % 2) * 8 + ((x + dx) % 4) * 2 + (core + dc) % 2)

    def at_depth(dz, dy):
        return (((y + dy) % 4) * 2 + (zh + dz) % 2, chan)

    near = [(0, 2), (0, 1), (0, 3)]
    far = [(1, 0), (1, 1), (1, 3), (1, 2)]
    moves = near + far
    deep = [(1, 2), (1, 1), (1, 3), (1, 0)]
    sibling = at_chan(0, 0, 1)

    def by_core(first, second):
        return [(a[0] + core * (b[0] - a[0]), a[1] + core * (b[1] - a[1])) for a, b in zip(first, second)]

    above = ((depth + 1) % 8, chan)
    below = ((depth + 7) % 8, chan)

    barrier = pltpu.get_barrier_semaphore()
    peers = [sibling] + [at_chan(*m) for m in moves] + [at_depth(*m) for m in moves]
    for peer in peers:
        pl.semaphore_signal(barrier, inc=1, device_id=peer, device_id_type=MESH)

    number = itertools.count()
    sent = []

    def push(src, dst, target):
        n = next(number)
        copy = pltpu.make_async_remote_copy(
            src_ref=src, dst_ref=dst, send_sem=send_sem.at[n], recv_sem=recv_sem.at[n],
            device_id=target, device_id_type=MESH,
        )
        copy.start()
        sent.append(copy)
        return copy

    def build(level, wide):
        for tap, phase, row_step, col_step in taps_2d():
            view = wide[:, phase * CELLS : (phase + 1) * CELLS]
            amount = -row_step * SIDE - col_step
            if amount:
                view = jnp.where(inside(row_step, col_step), pltpu.roll(view, amount, 1), 0.0)
            start = level * LEVEL + tap * INS
            views[start : start + INS, :] = view.astype(BF)

    loads[0].wait()
    unpack(vol, vol_rows)

    def plane(p):
        return take(vol_rows, INS, 4, p)

    top[...] = plane(3).astype(BF)
    pl.semaphore_wait(barrier, len(peers))
    halo = push(top, low, above)

    views[5 * LEVEL :, :] = jnp.zeros((views.shape[0] - 5 * LEVEL, CELLS), BF)
    for p in (1, 2, 3):
        build(p + 1, plane(p))

    loads[1].wait()
    for other in range(2):
        row = lax.broadcasted_iota(jnp.int32, (HALF, ALL), 0)
        channel = lax.broadcasted_iota(jnp.int32, (HALF, ALL), 1)
        z_rel, x_rel, within = row // (4 * OUTS), (row // OUTS) % 4, row % OUTS
        wanted = ((zl + z_rel) % 2) * HALF + ((x + x_rel) % 4) * (2 * OUTS) + ((core + other) % 2) * OUTS + within
        select = jnp.where(channel == wanted, 1.0, 0.0).astype(BF)
        wt[other, :, 0:ROWS] = dot(select, wk[...], ((1,), (1,))).astype(BF)
        wt[other, :, ROWS:DEEP] = jnp.zeros((HALF, DEEP - ROWS), BF)

    def partial(q, other):
        first = 2 * LEVEL * q
        return dot(wt[other], views[first : first + DEEP, :], ((1,), (0,)))

    def to_sibling(q):
        sib_out[q] = partial(q, 1).astype(BF)
        return push(sib_out.at[q], sib_in.at[q], sibling)

    def scatter(q, copy):
        copy.wait_recv()
        acc[q] = acc[q] + sib_in[q].astype(F32)
        rs_out[q] = acc[q].astype(BF)
        copies = []
        for n, (dz, dx) in enumerate(by_core(far + near, near + far)):
            start = pl.multiple_of((dz * 4 + dx) * OUTS, OUTS)
            copies.append(push(rs_out.at[q, pl.ds(start, OUTS), :], rs_in.at[q, n], at_chan(dz, dx)))
        return copies

    sib_1 = to_sibling(1)
    acc[1] = partial(1, 0)
    scatter_1 = scatter(1, sib_1)
    loads[2].wait()
    unpack(cot, cot_rows)
    build(1, plane(0))
    halo.wait_recv()
    build(0, jnp.where(depth > 0, low[...].astype(F32), 0.0))
    sib_0 = to_sibling(0)
    acc[0] = partial(0, 0)
    scatter_0 = scatter(0, sib_0)

    def rows_abs(dz, dx):
        return pl.multiple_of((((zl + dz) % 2) * 8 + ((x + dx) % 4) * 2 + core) * OUTS, OUTS)

    def activate(q, copies):
        for copy in copies:
            copy.wait_recv()
        preact = acc[q, 0:OUTS, :]
        for n in range(len(moves)):
            preact = preact + rs_in[q, n].astype(F32)
        s = 1.0 / (1.0 + jnp.exp(-preact))
        put(act_rows, OUTS, 2, q, 0, preact * s)
        grad = take(cot_rows, OUTS, 2, q) * s * (1.0 + preact * (1.0 - s))
        grads[q, pl.ds(rows_abs(0, 0), OUTS), :] = grad.astype(BF)

    def spread(q, start, target):
        place = grads.at[q, pl.ds(start, OUTS), :]
        return push(place, place, target)

    shared = {0: {}, 1: {}}

    def share(q, move):
        dz, dx = move
        shared[q][move] = spread(q, rows_abs(dz, -dx), sibling)

    pair = at_chan(1, 0)
    across = {}
    activate(1, scatter_1)
    near_1 = {move: spread(1, rows_abs(0, 0), at_chan(*move)) for move in near}
    across[1, 0] = spread(1, rows_abs(0, 0), pair)
    share(1, (0, 0))
    activate(0, scatter_0)
    across_0 = spread(0, rows_abs(0, 0), pair)
    near_0 = {move: spread(0, rows_abs(0, 0), at_chan(*move)) for move in near}
    share(0, (0, 0))
    for move in near:
        near_1[move].wait_recv()
        across[1, move[1]] = spread(1, rows_abs(0, -move[1]), pair)
        share(1, move)
    across_0.wait_recv()
    far_0 = {(1, dx): spread(0, rows_abs(1, 0), at_chan(0, dx)) for _, dx in near}
    share(0, (1, 0))
    across[1, 0].wait_recv()
    share(1, (1, 0))
    for move in near:
        near_0[move].wait_recv()
        share(0, move)
    for q in range(2):
        for move in [(0, 0)] + near:
            shared[q][move].wait_recv()
    pack(act_rows, act)
    save(act, act_hbm)

    def filters(part, z):
        columns = pl.ds(pl.multiple_of(z * HALF, HALF), HALF)
        total = dot(views[0:ROWS, :], grads[0, columns, :], ((1,), (1,))) + dot(
            views[2 * LEVEL : 2 * LEVEL + ROWS, :], grads[1, columns, :], ((1,), (1,))
        )
        for side in range(2):
            filt[part, side, 0:ROWS, :] = total[:, side * PART : (side + 1) * PART]
        filt[part, :, ROWS:, :] = jnp.zeros((2, 4 * PIECE - ROWS, PART), F32)
        filt_out[part] = filt[part].astype(BF)
        copies = []
        for n, (dz, dy) in enumerate(deep + near):
            start = pl.multiple_of(((y + dy) % 4) * PIECE, PIECE)
            src = filt_out.at[part, (zh + dz) % 2, pl.ds(start, PIECE), :]
            copies.append(push(src, filt_in.at[part, n], at_depth(dz, dy)))
        return copies

    def summed(part, z, copies):
        for copy in copies:
            copy.wait_recv()
        start = pl.multiple_of(y * PIECE, PIECE)
        total = filt[part, zh, pl.ds(start, PIECE), :]
        for n in range(len(moves)):
            total = total + filt_in[part, n].astype(F32)
        final[part] = total.astype(BF)
        place = gker_hbm.at[z, y, zh]
        save(final.at[part], place)
        return [push(final.at[part], place, at_depth(*move)) for move in by_core(far + near, near + far)]

    reduce_0 = filters(0, zl)
    for _, dx in near:
        across[1, dx].wait_recv()
        share(1, (1, dx))
        far_0[1, dx].wait_recv()
        share(0, (1, dx))
    for q in range(2):
        for move in far:
            shared[q][move].wait_recv()
    reduce_1 = filters(1, 1 - zl)
    spread_0 = summed(0, zl, reduce_0)

    def spatial(columns):
        sums = {}
        for tap, phase, row_step, col_step in taps_2d():
            moved = columns[tap * INS : (tap + 1) * INS, :]
            amount = -row_step * SIDE - col_step
            if amount:
                moved = pltpu.roll(jnp.where(inside(row_step, col_step), moved, 0.0), CELLS - amount, 1)
            sums[phase] = moved if phase not in sums else sums[phase] + moved
        return [sums[phase] for phase in range(4)]

    def columns_of(q, level):
        return spatial(dot(wk[level * LEVEL : (level + 1) * LEVEL, :], grads[q], ((1,), (0,))))

    def phase_cells(phase):
        return slice(phase * CELLS, (phase + 1) * CELLS)

    def store_plane(plane, parts, more=None):
        for phase in range(4):
            total = parts[phase] if more is None else parts[phase] + more[phase]
            put(gvol_rows, INS, 4, plane, phase * (CELLS // 128), total)

    lowest = columns_of(0, 0)
    for phase in range(4):
        back_out[:, phase_cells(phase)] = lowest[phase].astype(BF)
    back = push(back_out, upper, below)
    store_plane(0, columns_of(0, 1))
    store_plane(1, columns_of(0, 2), columns_of(1, 0))
    spread_1 = summed(1, 1 - zl, reduce_1)
    store_plane(2, columns_of(1, 1))
    last = columns_of(1, 2)
    back.wait_recv()
    edge = jnp.where(depth < 7, upper[...].astype(F32), 0.0)
    store_plane(3, last, [edge[:, phase_cells(phase)] for phase in range(4)])
    pack(gvol_rows, gvol)
    save(gvol, gvol_hbm)
    for copy in spread_0 + spread_1:
        copy.wait_recv()
    for copy in sent:
        copy.wait_send()
    for copy in saves:
        copy.wait()


def store(act, gvol, pieces, act_out, gvol_out, gker_out, act_in, gvol_in, pieces_in, gker, load_sem, save_sem):
    loads, saves = [], []

    def carry(src, dst, sems, copies):
        copy = pltpu.make_async_copy(src, dst, sems.at[len(copies)])
        copy.start()
        copies.append(copy)

    for z in range(2):
        carry(pieces.at[z], pieces_in.at[z], load_sem, loads)
    carry(gvol, gvol_in, load_sem, loads)
    carry(act, act_in, load_sem, loads)
    for z in range(2):
        loads[z].wait()
        for y in range(4):
            rows = min(PIECE, ROWS - y * PIECE)
            for side in range(2):
                first = z * HALF + side * PART
                gker[y * PIECE : y * PIECE + rows, first : first + PART] = pieces_in[z, y, side, :rows, :].astype(F32)
        columns = slice(z * HALF, (z + 1) * HALF)
        carry(gker.at[:, columns], gker_out.at[:, columns], save_sem, saves)
    loads[2].wait()
    carry(gvol_in, gvol_out, save_sem, saves)
    loads[3].wait()
    carry(act_in, act_out, save_sem, saves)
    for copy in saves:
        copy.wait()


def on_device(volume, kernel, cotangent):
    scratch = [
        (volume.shape, BF),
        ((ROWS, ALL), BF),
        (cotangent.shape, BF),
        (cotangent.shape, BF),
        (volume.shape, BF),
        ((INS, 4 * CELLS), BF),
        ((INS, 4 * CELLS), BF),
        ((INS, 4 * CELLS), BF),
        ((4 * INS * CELLS // 32 + 8, 128), F32),
        ((2 * OUTS * CELLS // 128 + 8, 128), F32),
        ((2 * OUTS * CELLS // 128 + 8, 128), F32),
        ((4 * INS * CELLS // 32 + 8, 128), F32),
        ((2 * LEVEL + DEEP, CELLS), BF),
        ((2, HALF, DEEP), BF),
        ((2, HALF, CELLS), BF),
        ((2, HALF, CELLS), BF),
        ((2, HALF, CELLS), F32),
        ((2, HALF, CELLS), BF),
        ((2, 7, OUTS, CELLS), BF),
        ((2, ALL, CELLS), BF),
        ((INS, 4 * CELLS), BF),
        ((2, 2, 4 * PIECE, PART), F32),
        ((2, 2, 4 * PIECE, PART), BF),
        ((2, 7, PIECE, PART), BF),
        ((2, PIECE, PART), BF),
    ]
    whole = pl.BlockSpec(memory_space=pl.ANY)
    activated, grad_volume, grad_kernel = pl.pallas_call(
        body,
        out_shape=(
            jax.ShapeDtypeStruct(cotangent.shape, BF),
            jax.ShapeDtypeStruct(volume.shape, BF),
            jax.ShapeDtypeStruct((2, 4, 2, PIECE, PART), BF),
        ),
        in_specs=[whole] * 3,
        out_specs=(whole,) * 3,
        scratch_shapes=[pltpu.VMEM(shape, kind) for shape, kind in scratch]
        + [pltpu.SemaphoreType.DMA((COPIES,)), pltpu.SemaphoreType.DMA((COPIES,)), pltpu.SemaphoreType.DMA((3,)), pltpu.SemaphoreType.DMA((4,))],
        compiler_params=pltpu.CompilerParams(
            collective_id=0, has_side_effects=True, vmem_limit_bytes=56 * 1024 * 1024
        ),
    )(volume, kernel.reshape(ROWS, ALL), cotangent)
    results = (activated, grad_volume, grad_kernel)
    activated, grad_volume, grad_kernel = pl.pallas_call(
        store,
        out_shape=(
            jax.ShapeDtypeStruct(cotangent.shape, BF),
            jax.ShapeDtypeStruct(volume.shape, BF),
            jax.ShapeDtypeStruct((ROWS, ALL), F32),
        ),
        in_specs=[whole] * 3,
        out_specs=(whole,) * 3,
        scratch_shapes=[pltpu.VMEM(r.shape, r.dtype) for r in results]
        + [pltpu.VMEM((ROWS, ALL), F32), pltpu.SemaphoreType.DMA((4,)), pltpu.SemaphoreType.DMA((4,))],
        compiler_params=pltpu.CompilerParams(vmem_limit_bytes=56 * 1024 * 1024),
    )(*results)
    return activated, grad_volume, grad_kernel.reshape(TAPS, INS, ALL)


def solution(mesh):
    return jax.shard_map(
        on_device,
        mesh=mesh,
        in_specs=(P("chan", "depth", None), P(None, "chan", None), P("chan", "depth", None)),
        out_specs=(P("chan", "depth", None), P("chan", "depth", None), P(None, "chan", None)),
        check_vma=False,
    )
```

```python
import itertools

import jax
import jax.numpy as jnp
from jax import lax
from jax.experimental import pallas as pl
from jax.experimental.pallas import tpu as pltpu
from jax.sharding import PartitionSpec as P

MESH = pl.DeviceIdType.MESH
BF = jnp.bfloat16
F32 = jnp.float32
SIDE = 32
CELLS = SIDE * SIDE
TAPS = 27
INS = 16
OUTS = 32
ROWS = TAPS * INS
LEVEL = 9 * INS
DEEP = 512
ALL = 512
HALF = ALL // 2
PIECE = 112
PART = 128
COPIES = 80


def tap_phase(offset):
    if offset == 1:
        return (0, 0)
    if offset == 2:
        return (1, 0)
    return (1, -1)


def taps_2d():
    for row in range(3):
        for col in range(3):
            row_phase, row_step = tap_phase(row)
            col_phase, col_step = tap_phase(col)
            yield 3 * row + col, 2 * row_phase + col_phase, row_step, col_step


def inside(row_step, col_step):
    places = lax.broadcasted_iota(jnp.int32, (INS, CELLS), 1)
    keep = None
    if row_step:
        keep = places >= SIDE
    if col_step:
        col = (places % SIDE) != 0
        keep = col if keep is None else keep & col
    return keep


def unpack(src, rows):
    count, group, width = src.shape
    for tile in range(width // 128):
        size = count * group
        block = src[:, :, tile * 128 : tile * 128 + 128].astype(F32)
        rows[tile * size : tile * size + size, :] = block.reshape(size, 128)


def take(rows, count, group, place):
    size = count * group
    tiles = [rows[pl.ds(tile * size + place, count, stride=group), :] for tile in range(rows.shape[0] // size)]
    return jnp.concatenate(tiles, axis=1)


def put(rows, count, group, place, first, value):
    size = count * group
    for tile in range(value.shape[1] // 128):
        start = (first + tile) * size + place
        rows[pl.ds(start, count, stride=group), :] = value[:, tile * 128 : tile * 128 + 128]


def pack(rows, dst):
    count, group, width = dst.shape
    for tile in range(width // 128):
        size = count * group
        block = rows[tile * size : tile * size + size, :].reshape(count, group, 128)
        dst[:, :, tile * 128 : tile * 128 + 128] = block.astype(BF)


def dot(left, right, contract):
    return lax.dot_general(left, right, (contract, ((), ())), preferred_element_type=F32)


def body(
    vol_hbm, wk_hbm, cot_hbm, act_hbm, gvol_hbm, gker_hbm,
    vol, wk, cot, act, gvol,
    low, upper, top, vol_rows, cot_rows, act_rows, gvol_rows, views, wt, sib_out, sib_in, acc, rs_out, rs_in,
    grads, back_out, filt, filt_out, filt_in, final,
    send_sem, recv_sem, load_sem, save_sem,
):
    loads = [
        pltpu.make_async_copy(src, dst, load_sem.at[n])
        for n, (src, dst) in enumerate(((vol_hbm, vol), (wk_hbm, wk), (cot_hbm, cot)))
    ]
    for load in loads:
        load.start()
    saves = []

    def save(src, dst):
        copy = pltpu.make_async_copy(src, dst, save_sem.at[len(saves)])
        copy.start()
        saves.append(copy)

    depth = lax.axis_index("depth")
    chan = lax.axis_index("chan")
    y, zh = depth // 2, depth % 2
    zl, x, core = chan // 8, (chan // 2) % 4, chan % 2

    def at_chan(dz, dx, dc=0):
        return (depth, ((zl + dz) % 2) * 8 + ((x + dx) % 4) * 2 + (core + dc) % 2)

    def at_depth(dz, dy):
        return (((y + dy) % 4) * 2 + (zh + dz) % 2, chan)

    near = [(0, 2), (0, 1), (0, 3)]
    far = [(1, 0), (1, 1), (1, 3), (1, 2)]
    moves = near + far
    deep = [(1, 2), (1, 1), (1, 3), (1, 0)]
    sibling = at_chan(0, 0, 1)

    def by_core(first, second):
        return [(a[0] + core * (b[0] - a[0]), a[1] + core * (b[1] - a[1])) for a, b in zip(first, second)]

    above = ((depth + 1) % 8, chan)
    below = ((depth + 7) % 8, chan)

    barrier = pltpu.get_barrier_semaphore()
    peers = [sibling] + [at_chan(*m) for m in moves] + [at_depth(*m) for m in moves]
    for peer in peers:
        pl.semaphore_signal(barrier, inc=1, device_id=peer, device_id_type=MESH)

    number = itertools.count()
    sent = []

    def push(src, dst, target):
        n = next(number)
        copy = pltpu.make_async_remote_copy(
            src_ref=src, dst_ref=dst, send_sem=send_sem.at[n], recv_sem=recv_sem.at[n],
            device_id=target, device_id_type=MESH,
        )
        copy.start()
        sent.append(copy)
        return copy

    def build(level, wide):
        for tap, phase, row_step, col_step in taps_2d():
            view = wide[:, phase * CELLS : (phase + 1) * CELLS]
            amount = -row_step * SIDE - col_step
            if amount:
                view = jnp.where(inside(row_step, col_step), pltpu.roll(view, amount, 1), 0.0)
            start = level * LEVEL + tap * INS
            views[start : start + INS, :] = view.astype(BF)

    loads[0].wait()
    unpack(vol, vol_rows)

    def plane(p):
        return take(vol_rows, INS, 4, p)

    top[...] = plane(3).astype(BF)
    pl.semaphore_wait(barrier, len(peers))
    halo = push(top, low, above)

    views[5 * LEVEL :, :] = jnp.zeros((views.shape[0] - 5 * LEVEL, CELLS), BF)
    for p in (1, 2, 3):
        build(p + 1, plane(p))

    loads[1].wait()
    for other in range(2):
        row = lax.broadcasted_iota(jnp.int32, (HALF, ALL), 0)
        channel = lax.broadcasted_iota(jnp.int32, (HALF, ALL), 1)
        z_rel, x_rel, within = row // (4 * OUTS), (row // OUTS) % 4, row % OUTS
        wanted = ((zl + z_rel) % 2) * HALF + ((x + x_rel) % 4) * (2 * OUTS) + ((core + other) % 2) * OUTS + within
        select = jnp.where(channel == wanted, 1.0, 0.0).astype(BF)
        wt[other, :, 0:ROWS] = dot(select, wk[...], ((1,), (1,))).astype(BF)
        wt[other, :, ROWS:DEEP] = jnp.zeros((HALF, DEEP - ROWS), BF)

    def partial(q, other):
        first = 2 * LEVEL * q
        return dot(wt[other], views[first : first + DEEP, :], ((1,), (0,)))

    def to_sibling(q):
        sib_out[q] = partial(q, 1).astype(BF)
        return push(sib_out.at[q], sib_in.at[q], sibling)

    def scatter(q, copy):
        copy.wait_recv()
        acc[q] = acc[q] + sib_in[q].astype(F32)
        rs_out[q] = acc[q].astype(BF)
        copies = []
        for n, (dz, dx) in enumerate(by_core(far + near, near + far)):
            start = pl.multiple_of((dz * 4 + dx) * OUTS, OUTS)
            copies.append(push(rs_out.at[q, pl.ds(start, OUTS), :], rs_in.at[q, n], at_chan(dz, dx)))
        return copies

    sib_1 = to_sibling(1)
    acc[1] = partial(1, 0)
    scatter_1 = scatter(1, sib_1)
    loads[2].wait()
    unpack(cot, cot_rows)
    build(1, plane(0))
    halo.wait_recv()
    build(0, jnp.where(depth > 0, low[...].astype(F32), 0.0))
    sib_0 = to_sibling(0)
    acc[0] = partial(0, 0)
    scatter_0 = scatter(0, sib_0)

    def rows_abs(dz, dx):
        return pl.multiple_of((((zl + dz) % 2) * 8 + ((x + dx) % 4) * 2 + core) * OUTS, OUTS)

    def activate(q, copies):
        for copy in copies:
            copy.wait_recv()
        preact = acc[q, 0:OUTS, :]
        for n in range(len(moves)):
            preact = preact + rs_in[q, n].astype(F32)
        s = 1.0 / (1.0 + jnp.exp(-preact))
        put(act_rows, OUTS, 2, q, 0, preact * s)
        grad = take(cot_rows, OUTS, 2, q) * s * (1.0 + preact * (1.0 - s))
        grads[q, pl.ds(rows_abs(0, 0), OUTS), :] = grad.astype(BF)

    def spread(q, start, target):
        place = grads.at[q, pl.ds(start, OUTS), :]
        return push(place, place, target)

    shared = {0: {}, 1: {}}

    def share(q, move):
        dz, dx = move
        shared[q][move] = spread(q, rows_abs(dz, -dx), sibling)

    pair = at_chan(1, 0)
    across = {}
    activate(1, scatter_1)
    near_1 = {move: spread(1, rows_abs(0, 0), at_chan(*move)) for move in near}
    across[1, 0] = spread(1, rows_abs(0, 0), pair)
    share(1, (0, 0))
    activate(0, scatter_0)
    across_0 = spread(0, rows_abs(0, 0), pair)
    near_0 = {move: spread(0, rows_abs(0, 0), at_chan(*move)) for move in near}
    share(0, (0, 0))
    for move in near:
        near_1[move].wait_recv()
        across[1, move[1]] = spread(1, rows_abs(0, -move[1]), pair)
        share(1, move)
    across_0.wait_recv()
    far_0 = {(1, dx): spread(0, rows_abs(1, 0), at_chan(0, dx)) for _, dx in near}
    share(0, (1, 0))
    across[1, 0].wait_recv()
    share(1, (1, 0))
    for move in near:
        near_0[move].wait_recv()
        share(0, move)
    for q in range(2):
        for move in [(0, 0)] + near:
            shared[q][move].wait_recv()
    pack(act_rows, act)
    save(act, act_hbm)

    def filters(part, z):
        columns = pl.ds(pl.multiple_of(z * HALF, HALF), HALF)
        total = dot(views[0:ROWS, :], grads[0, columns, :], ((1,), (1,))) + dot(
            views[2 * LEVEL : 2 * LEVEL + ROWS, :], grads[1, columns, :], ((1,), (1,))
        )
        for side in range(2):
            filt[part, side, 0:ROWS, :] = total[:, side * PART : (side + 1) * PART]
        filt[part, :, ROWS:, :] = jnp.zeros((2, 4 * PIECE - ROWS, PART), F32)
        copies = []
        for dz, group in ((1, deep), (0, near)):
            half = (zh + dz) % 2
            filt_out[part, half] = filt[part, half].astype(BF)
            for _, dy in group:
                start = pl.multiple_of(((y + dy) % 4) * PIECE, PIECE)
                src = filt_out.at[part, half, pl.ds(start, PIECE), :]
                copies.append(push(src, filt_in.at[part, len(copies)], at_depth(dz, dy)))
        return copies

    def summed(part, z, copies):
        for copy in copies:
            copy.wait_recv()
        start = pl.multiple_of(y * PIECE, PIECE)
        total = filt[part, zh, pl.ds(start, PIECE), :]
        for n in range(len(moves)):
            total = total + filt_in[part, n].astype(F32)
        final[part] = total.astype(BF)
        place = gker_hbm.at[z, y, zh]
        save(final.at[part], place)
        return [push(final.at[part], place, at_depth(*move)) for move in by_core(far + near, near + far)]

    reduce_0 = filters(0, zl)
    for _, dx in near:
        across[1, dx].wait_recv()
        share(1, (1, dx))
        far_0[1, dx].wait_recv()
        share(0, (1, dx))
    for q in range(2):
        for move in far:
            shared[q][move].wait_recv()
    reduce_1 = filters(1, 1 - zl)
    spread_0 = summed(0, zl, reduce_0)

    def spatial(columns):
        sums = {}
        for tap, phase, row_step, col_step in taps_2d():
            moved = columns[tap * INS : (tap + 1) * INS, :]
            amount = -row_step * SIDE - col_step
            if amount:
                moved = pltpu.roll(jnp.where(inside(row_step, col_step), moved, 0.0), CELLS - amount, 1)
            sums[phase] = moved if phase not in sums else sums[phase] + moved
        return [sums[phase] for phase in range(4)]

    def columns_of(q, level):
        return spatial(dot(wk[level * LEVEL : (level + 1) * LEVEL, :], grads[q], ((1,), (0,))))

    def phase_cells(phase):
        return slice(phase * CELLS, (phase + 1) * CELLS)

    def store_plane(plane, parts, more=None):
        for phase in range(4):
            total = parts[phase] if more is None else parts[phase] + more[phase]
            put(gvol_rows, INS, 4, plane, phase * (CELLS // 128), total)

    lowest = columns_of(0, 0)
    for phase in range(4):
        back_out[:, phase_cells(phase)] = lowest[phase].astype(BF)
    back = push(back_out, upper, below)
    store_plane(0, columns_of(0, 1))
    store_plane(1, columns_of(0, 2), columns_of(1, 0))
    spread_1 = summed(1, 1 - zl, reduce_1)
    store_plane(2, columns_of(1, 1))
    last = columns_of(1, 2)
    back.wait_recv()
    edge = jnp.where(depth < 7, upper[...].astype(F32), 0.0)
    store_plane(3, last, [edge[:, phase_cells(phase)] for phase in range(4)])
    pack(gvol_rows, gvol)
    save(gvol, gvol_hbm)
    for copy in spread_0 + spread_1:
        copy.wait_recv()
    for copy in sent:
        copy.wait_send()
    for copy in saves:
        copy.wait()


def store(act, gvol, pieces, act_out, gvol_out, gker_out, act_in, gvol_in, pieces_in, gker, load_sem, save_sem):
    loads, saves = [], []

    def carry(src, dst, sems, copies):
        copy = pltpu.make_async_copy(src, dst, sems.at[len(copies)])
        copy.start()
        copies.append(copy)

    for z in range(2):
        carry(pieces.at[z], pieces_in.at[z], load_sem, loads)
    carry(gvol, gvol_in, load_sem, loads)
    carry(act, act_in, load_sem, loads)
    for z in range(2):
        loads[z].wait()
        for y in range(4):
            rows = min(PIECE, ROWS - y * PIECE)
            for side in range(2):
                first = z * HALF + side * PART
                gker[y * PIECE : y * PIECE + rows, first : first + PART] = pieces_in[z, y, side, :rows, :].astype(F32)
        columns = slice(z * HALF, (z + 1) * HALF)
        carry(gker.at[:, columns], gker_out.at[:, columns], save_sem, saves)
    loads[2].wait()
    carry(gvol_in, gvol_out, save_sem, saves)
    loads[3].wait()
    carry(act_in, act_out, save_sem, saves)
    for copy in saves:
        copy.wait()


def on_device(volume, kernel, cotangent):
    scratch = [
        (volume.shape, BF),
        ((ROWS, ALL), BF),
        (cotangent.shape, BF),
        (cotangent.shape, BF),
        (volume.shape, BF),
        ((INS, 4 * CELLS), BF),
        ((INS, 4 * CELLS), BF),
        ((INS, 4 * CELLS), BF),
        ((4 * INS * CELLS // 32 + 8, 128), F32),
        ((2 * OUTS * CELLS // 128 + 8, 128), F32),
        ((2 * OUTS * CELLS // 128 + 8, 128), F32),
        ((4 * INS * CELLS // 32 + 8, 128), F32),
        ((2 * LEVEL + DEEP, CELLS), BF),
        ((2, HALF, DEEP), BF),
        ((2, HALF, CELLS), BF),
        ((2, HALF, CELLS), BF),
        ((2, HALF, CELLS), F32),
        ((2, HALF, CELLS), BF),
        ((2, 7, OUTS, CELLS), BF),
        ((2, ALL, CELLS), BF),
        ((INS, 4 * CELLS), BF),
        ((2, 2, 4 * PIECE, PART), F32),
        ((2, 2, 4 * PIECE, PART), BF),
        ((2, 7, PIECE, PART), BF),
        ((2, PIECE, PART), BF),
    ]
    whole = pl.BlockSpec(memory_space=pl.ANY)
    activated, grad_volume, grad_kernel = pl.pallas_call(
        body,
        out_shape=(
            jax.ShapeDtypeStruct(cotangent.shape, BF),
            jax.ShapeDtypeStruct(volume.shape, BF),
            jax.ShapeDtypeStruct((2, 4, 2, PIECE, PART), BF),
        ),
        in_specs=[whole] * 3,
        out_specs=(whole,) * 3,
        scratch_shapes=[pltpu.VMEM(shape, kind) for shape, kind in scratch]
        + [pltpu.SemaphoreType.DMA((COPIES,)), pltpu.SemaphoreType.DMA((COPIES,)), pltpu.SemaphoreType.DMA((3,)), pltpu.SemaphoreType.DMA((4,))],
        compiler_params=pltpu.CompilerParams(
            collective_id=0, has_side_effects=True, vmem_limit_bytes=56 * 1024 * 1024
        ),
    )(volume, kernel.reshape(ROWS, ALL), cotangent)
    results = (activated, grad_volume, grad_kernel)
    activated, grad_volume, grad_kernel = pl.pallas_call(
        store,
        out_shape=(
            jax.ShapeDtypeStruct(cotangent.shape, BF),
            jax.ShapeDtypeStruct(volume.shape, BF),
            jax.ShapeDtypeStruct((ROWS, ALL), F32),
        ),
        in_specs=[whole] * 3,
        out_specs=(whole,) * 3,
        scratch_shapes=[pltpu.VMEM(r.shape, r.dtype) for r in results]
        + [pltpu.VMEM((ROWS, ALL), F32), pltpu.SemaphoreType.DMA((4,)), pltpu.SemaphoreType.DMA((4,))],
        compiler_params=pltpu.CompilerParams(vmem_limit_bytes=56 * 1024 * 1024),
    )(*results)
    return activated, grad_volume, grad_kernel.reshape(TAPS, INS, ALL)


def solution(mesh):
    return jax.shard_map(
        on_device,
        mesh=mesh,
        in_specs=(P("chan", "depth", None), P(None, "chan", None), P("chan", "depth", None)),
        out_specs=(P("chan", "depth", None), P("chan", "depth", None), P(None, "chan", None)),
        check_vma=False,
    )
```
